32 devices in a mesh: img: 4 (over y, x), ori: 8 (over z, core).
Axes of the slice: x: 2, y: 2, z: 4, core: 2. Of those that a mesh axis runs over, the one named last changes fastest.
Arguments:
- images: bfloat16 [8192, 2048], P(('img', 'ori')), may hold values from -128 to 128, as said below
- projections: bfloat16 [8192, 2048], P('ori'), may hold values from -1 to 1
- brick_dest: int32 [8192, 16, 1], P('ori'), may hold values from 0 to 31; in each aligned block of 4096 rows (0 to 4095, 4096 to 8191, ..., all dimensions but the last counted through in order) at most 256 rows name the same one
- brick_rows: int32 [8192, 16], P('ori'), may hold values from 0 to 255
- kernel: bfloat16 [32, 128, 128], P(('img', 'ori')), may hold values from -3 to 3
Outputs:
- data_volume: float32 [32, 256, 128], P(('img', 'ori'))
- weight_volume: float32 [32, 256], P(('img', 'ori'))
The draws below stay inside these ranges and needn't reach their ends.
Inputs may be any that keep to these rules, and one draw needn't show every extreme that they name: `images`: images may be large where an image nearly equals reference projections. `brick_dest`: in each aligned block of 4096 segments (the slices one device owns, in order of orientation and segment) at most 256 segments name the same brick, and some block reaches 256.
All inputs are finite; a program needn't handle non-finite values.
Results may differ from the reference program's by a relative error of at most 0.0027.
Values may be sent and summed in bfloat16 or wider, within the bound.
No kernel may reach another device: no remote copies, remote signals or barrier semaphores. Data moves between devices by JAX's collectives and lax.ppermute only.
A program may use at most 128 MiB of HBM per device.

```python
import math
import jax
import jax.numpy as jnp
import numpy as np
from jax import lax

F = 2048
SEG = 128
NSEG = 16
IMG_DEV = 2048
BRICK_ROWS = 256
IMAGES = 8192
ORIENTS = 8192
SEGS_DEV = 4096
BRICKS = 32
CAP = 256


def projection_normals(key):
    subkey = jax.random.fold_in(key, 11)
    return jax.random.normal(subkey, (ORIENTS, F), jnp.float32) / jnp.sqrt(jnp.float32(F))


def draw_projections(key, part):
    normals = projection_normals(key)
    return normals.astype(jnp.bfloat16)


def draw_images(key, part):
    peaks = jax.random.randint(jax.random.fold_in(key, 21), (IMAGES,), 0, ORIENTS)
    amplitude = (jnp.log(jnp.float32(ORIENTS)) - 0.5) / 4.0
    chosen = projection_normals(key)[peaks]
    signal = amplitude * chosen
    common = 0.1 * jax.random.normal(jax.random.fold_in(key, 22), (1, F), jnp.float32)
    noise = 0.08 * jnp.clip(jax.random.normal(jax.random.fold_in(key, 23), (IMAGES, F), jnp.float32), -6.0, 6.0)
    values = signal + common + noise
    return values.astype(jnp.bfloat16)


def draw_kernel(key, part):
    subkey = jax.random.fold_in(key, 31)
    normals = jax.random.normal(subkey, (BRICKS, SEG, SEG), jnp.float32) * (0.5 / jnp.sqrt(jnp.float32(SEG)))
    return (normals + jnp.eye(SEG, dtype=jnp.float32)[None, :, :]).astype(jnp.bfloat16)


def touch_ends(drawn, key, low, high):
    longest = drawn.shape.index(max(drawn.shape))
    spots = []
    for shift in (0, 1):
        where = [jax.random.randint(jax.random.fold_in(key, axis), (), 0, length) for axis, length in enumerate(drawn.shape)]
        where[longest] = (where[longest] + shift) % drawn.shape[longest]
        spots.append(tuple(where))
    return drawn.at[spots[0]].set(low).at[spots[1]].set(high)


def routed_block(stream_key, own, number, rows, amount, top, limit, lean):
    ranking = jax.random.permutation(stream_key, amount)
    heavy_load, usual = portions_of(amount, rows * top, limit, lean, True), portions_of(amount, rows * top, limit, lean, False)
    places = jnp.arange(amount)

    def named(sizes, rotation):
        used = int((sizes > 0).sum())
        fixed = max(1, used // 4)
        shifted = fixed + (places - fixed + rotation * (used - fixed)) % max(1, amount - fixed)
        return jnp.zeros((amount,), jnp.int32).at[ranking[jnp.where(places < fixed, places, shifted)]].set(jnp.asarray(sizes, jnp.int32))

    sizes = jnp.where(number % 4 == 0, named(heavy_load, number // 4), named(usual, number - number // 4 - 1))
    mixed = jax.random.permutation(jax.random.fold_in(own, 3), amount)
    giver, sink = mixed[0:amount // 2 * 2:2], mixed[1:amount // 2 * 2:2]
    margin = jnp.minimum(sizes[giver] - 1, limit - sizes[sink]) // 2
    margin = jnp.where((giver == ranking[0]) | (sink == ranking[0]) | (sizes[sink] == 0), 0, jnp.maximum(margin, 0))
    shifted = jax.random.randint(jax.random.fold_in(own, 4), (amount // 2,), 0, 1 << 20) % (margin + 1)
    sizes = sizes.at[giver].add(-shifted).at[sink].add(shifted)
    labels = jnp.searchsorted(jnp.cumsum(sizes), jnp.arange(rows * top), side="right").astype(jnp.int32)
    grid = labels.reshape(top, rows).T
    grid = grid[jax.random.permutation(jax.random.fold_in(own, 1), rows)]
    rotation = jax.random.randint(jax.random.fold_in(own, 2), (rows, 1), 0, top)
    return jnp.take_along_axis(grid, (jnp.arange(top)[None, :] + rotation) % top, axis=1)


def portions_of(number_of, total, most, lean, full):
    portions = [(1 << 20) // math.isqrt(grade ** lean) + 1 for grade in range(1, number_of + 1)]
    largest = most if full else min(most, max(-(-total // number_of), total * portions[0] // sum(portions)))
    least = 1 if total - largest >= number_of - 1 else 0
    holding, spare = [largest] + [least] * (number_of - 1), total - largest - least * (number_of - 1)
    while spare > 0:
        movable = [i for i in range(1, number_of) if holding[i] < largest] or [i for i in range(1, number_of) if holding[i] < most]
        mass, budget = sum([portions[i] for i in movable]), spare
        for i in movable:
            more = min(most - holding[i], max(1, budget * portions[i] // mass), spare)
            holding[i] = holding[i] + more
            spare = spare - more
    return np.array(holding)


def setup_inputs(seed: int = 0) -> dict:
    streams_of = jax.random.split(jax.random.key(seed), 6)
    images = draw_images(jax.random.fold_in(streams_of[5], 71), 0)
    projections = draw_projections(jax.random.fold_in(streams_of[5], 71), 0)
    brick_dest_keys = jax.random.split(jax.random.fold_in(streams_of[2], 1), ORIENTS * NSEG // SEGS_DEV)
    brick_dest_turns = jax.random.permutation(jax.random.fold_in(streams_of[2], 3), ORIENTS * NSEG // SEGS_DEV)
    brick_dest = jax.vmap(lambda own, number: routed_block(jax.random.fold_in(streams_of[2], 2), own, number, SEGS_DEV, BRICKS, 1, CAP, 2))(brick_dest_keys, brick_dest_turns).reshape((ORIENTS, NSEG, 1))
    brick_rows = touch_ends(jax.random.randint(streams_of[3], (ORIENTS, NSEG), 0, BRICK_ROWS), jax.random.fold_in(streams_of[3], 1), 0, BRICK_ROWS - 1).astype(jnp.int32)
    kernel = draw_kernel(jax.random.fold_in(streams_of[5], 71), 0)
    return {"images": images, "projections": projections, "brick_dest": brick_dest, "brick_rows": brick_rows, "kernel": kernel}


temper_scale = 4.0


def reference(images, projections, brick_dest, brick_rows, kernel):
    squared_norm = jnp.sum(jnp.square(projections.astype(jnp.float32)), axis=1)
    block_rows = min(512, IMG_DEV)
    blocks = images.reshape(IMAGES // block_rows, block_rows, F)

    def accumulate(running, image_block):
        slice_sums, weight_sums = running
        correlation = lax.dot_general(image_block, projections, (((1,), (1,)), ((), ())), preferred_element_type=jnp.float32)
        scores = temper_scale * (correlation - 0.5 * squared_norm[None, :])
        largest = jnp.max(scores, axis=1, keepdims=True)
        exponentials = jnp.exp(scores - largest)
        weights = exponentials / jnp.sum(exponentials, axis=1, keepdims=True)
        rounded = weights.astype(jnp.bfloat16)
        slice_sums = slice_sums + lax.dot_general(rounded, image_block, (((0,), (0,)), ((), ())), preferred_element_type=jnp.float32)
        weight_sums = weight_sums + jnp.sum(weights, axis=0)
        return (slice_sums, weight_sums), None

    start = (jnp.zeros((ORIENTS, F), jnp.float32), jnp.zeros((ORIENTS,), jnp.float32))
    (slice_sums, weight_sums), ignored = lax.scan(accumulate, start, blocks)
    slice_rounded = lax.optimization_barrier(slice_sums.astype(jnp.bfloat16)).astype(jnp.float32)
    weight_rounded = lax.optimization_barrier(weight_sums.astype(jnp.bfloat16)).astype(jnp.float32)
    segments = slice_rounded.reshape(ORIENTS * NSEG, SEG)
    segment_weights = jnp.repeat(weight_rounded, NSEG)
    target = (brick_dest.reshape(-1) * BRICK_ROWS + brick_rows.reshape(-1)).astype(jnp.int32)
    gridded = jax.ops.segment_sum(segments, target, num_segments=BRICKS * BRICK_ROWS).reshape(BRICKS, BRICK_ROWS, SEG)
    data_volume = jnp.einsum("brk,bkj->brj", gridded, kernel.astype(jnp.float32), precision=lax.Precision.HIGHEST)
    weight_volume = jax.ops.segment_sum(segment_weights, target, num_segments=BRICKS * BRICK_ROWS).reshape(BRICKS, BRICK_ROWS)
    return data_volume, weight_volume
```

```python
import functools

import jax
import jax.numpy as jnp
from jax import lax
from jax.experimental import pallas as pl
from jax.experimental.pallas import tpu as pltpu
from jax.sharding import PartitionSpec as P

BRICK_ROWS = 256
EXTRA_ROWS = 16
TILE = 256
temper_scale = 4.0

ANY = pl.BlockSpec(memory_space=pl.ANY)
VMEM = pl.BlockSpec(memory_space=pltpu.VMEM)
SMEM = pl.BlockSpec(memory_space=pltpu.SMEM)
NN = (((1,), (0,)), ((), ()))
NT = (((1,), (1,)), ((), ()))


def dot(a, b, dims=NN):
    return lax.dot_general(a, b, dims, preferred_element_type=jnp.float32)


def one_hot_rows(count, row):
    numbers = lax.broadcasted_iota(jnp.int32, (count, row.shape[1]), 0)
    return jnp.where(numbers == row, 1.0, 0.0).astype(jnp.bfloat16)


def place_kernel(bricks, groups, capacity, dest_ref, rows_ref, slot_ref, map_ref):
    width = dest_ref.shape[2]
    segments = dest_ref.shape[0] // groups
    room = map_ref.shape[2]
    upper = (
        lax.broadcasted_iota(jnp.int32, (width, width), 0)
        <= lax.broadcasted_iota(jnp.int32, (width, width), 1)
    )
    upper = jnp.where(upper, 1.0, 0.0).astype(jnp.bfloat16)
    ones = jnp.ones((width, width), jnp.bfloat16)

    def group(g, ignored):
        def segment(s, carry):
            taken, row_map = carry
            dest = dest_ref[g * segments + s]
            member = one_hot_rows(bricks, dest)
            count = dot(member, upper) + taken
            rank = jnp.sum(member.astype(jnp.float32) * count, axis=0, keepdims=True) - 1.0
            rank = rank.astype(jnp.int32)
            slot_ref[g * segments + s] = (dest * groups + g) * capacity + rank
            marked = member.astype(jnp.float32) * (rows_ref[g * segments + s] + 1).astype(
                jnp.float32
            )
            row_map += dot(marked.astype(jnp.bfloat16), one_hot_rows(room, rank), NT)
            return taken + dot(member, ones), row_map

        start = (jnp.zeros((bricks, width), jnp.float32), jnp.zeros((bricks, room), jnp.float32))
        taken, row_map = lax.fori_loop(0, segments, segment, start)
        map_ref[g] = row_map.astype(jnp.int32) - 1
        return ignored

    lax.fori_loop(0, groups, group, 0)


def score_kernel(chips, candidates, first, *refs):
    n = len(candidates)
    images, refs = refs[:n], refs[n:]
    proj_ref, refs = refs[0], refs[1:]
    if not first:
        norm_in, refs = refs[0], refs[4:]
    if first:
        norm_ref, refs = refs[0], refs[1:]
    else:
        norm_ref = norm_in
    p_hbm, x_hbm, stat_hbm, held, p_buf, stat_buf, sem_in, sem_p, sem_x, sem_s = refs
    block = held.shape[1]
    orients = proj_ref.shape[0]
    chunk = min(256, orients)
    me = lax.axis_index("ori")
    chip, core = me // 2, lax.rem(me, 2)
    plan = []
    for shift, other in candidates:
        source = chip + shift
        valid = jnp.logical_and(source >= 0, source < chips)
        plan.append((valid, jnp.clip(source, 0, chips - 1) * 2 + (1 - core if other else core)))

    def copies(i):
        slot = plan[i][1]
        rows = pl.ds(pl.multiple_of(slot * block, block), block)
        return (
            lambda: pltpu.make_async_copy(images[i], held.at[i], sem_in.at[i]),
            lambda: pltpu.make_async_copy(held.at[i], x_hbm.at[rows], sem_x.at[i]),
            lambda: pltpu.make_async_copy(p_buf.at[i], p_hbm.at[slot], sem_p.at[i]),
            lambda: pltpu.make_async_copy(stat_buf.at[i], stat_hbm.at[slot], sem_s.at[i]),
        )

    for i in range(n):

        @pl.when(plan[i][0])
        def _(i=i):
            copies(i)[0]().start()

    if first:

        def square(r, ignored):
            rows = pl.ds(pl.multiple_of(r * chunk, chunk), chunk)
            values = proj_ref[rows, :].astype(jnp.float32)
            total = jnp.sum(values * values, axis=1, keepdims=True)
            norm_ref[rows, :] = jnp.broadcast_to(total, (chunk, norm_ref.shape[1]))
            return ignored

        lax.fori_loop(0, orients // chunk, square, 0)

    for i in range(n):

        @pl.when(plan[i][0])
        def _(i=i):
            fetch, keep, out, stats = copies(i)
            fetch().wait()
            keep().start()

            def score(r, largest):
                rows = pl.ds(pl.multiple_of(r * chunk, chunk), chunk)
                found = dot(proj_ref[rows, :], held[i], NT)
                norm = norm_ref[rows, 0:1]
                found = temper_scale * (found - 0.5 * norm)
                p_buf[i, rows, :] = found
                return jnp.maximum(largest, jnp.max(found, axis=0, keepdims=True))

            largest = lax.fori_loop(
                0, orients // chunk, score, jnp.full((1, block), -jnp.inf, jnp.float32)
            )

            def exponential(r, total):
                rows = pl.ds(pl.multiple_of(r * chunk, chunk), chunk)
                value = jnp.exp(p_buf[i, rows, :] - largest)
                p_buf[i, rows, :] = value
                return total + jnp.sum(value, axis=0, keepdims=True)

            total = lax.fori_loop(
                0, orients // chunk, exponential, jnp.zeros((1, block), jnp.float32)
            )
            out().start()
            pick = lax.broadcasted_iota(jnp.int32, (8, block), 0) == 0
            stat_buf[i] = jnp.where(pick, largest, total)
            stats().start()

    for i in range(n):

        @pl.when(plan[i][0])
        def _(i=i):
            for copy in copies(i)[1:]:
                copy().wait()


def score_step(chips, candidates, images, projections, carry):
    block, width = images[0].shape
    orients = projections.shape[0]
    blocks = 2 * chips
    n = len(images)
    first = carry is None
    shapes = [
        jax.ShapeDtypeStruct((blocks, orients, block), jnp.float32),
        jax.ShapeDtypeStruct((blocks * block, width), jnp.bfloat16),
        jax.ShapeDtypeStruct((blocks, 8, block), jnp.float32),
    ]
    in_specs = [ANY] * n + [VMEM]
    args = list(images) + [projections]
    if first:
        out_shape = [jax.ShapeDtypeStruct((orients, 128), jnp.float32)] + shapes
        out_specs = [VMEM] + [ANY] * 3
        aliases = {}
    else:
        in_specs += [VMEM] + [ANY] * 3
        args += list(carry)
        out_shape, out_specs = shapes, [ANY] * 3
        aliases = {n + 2 + k: k for k in range(3)}
    out = pl.pallas_call(
        functools.partial(score_kernel, chips, candidates, first),
        out_shape=out_shape,
        in_specs=in_specs,
        out_specs=out_specs,
        scratch_shapes=[
            pltpu.VMEM((n, block, width), jnp.bfloat16),
            pltpu.VMEM((n, orients, block), jnp.float32),
            pltpu.VMEM((n, 8, block), jnp.float32),
            pltpu.SemaphoreType.DMA((n,)),
            pltpu.SemaphoreType.DMA((n,)),
            pltpu.SemaphoreType.DMA((n,)),
            pltpu.SemaphoreType.DMA((n,)),
        ],
        input_output_aliases=aliases,
        compiler_params=pltpu.CompilerParams(vmem_limit_bytes=40 << 20),
        cost_estimate=pl.CostEstimate(
            flops=2 * n * block * orients * width, bytes_accessed=n * (4 << 20), transcendentals=0
        ),
        name="score_blocks",
    )(*args)
    return tuple(out) if first else (carry[0],) + tuple(out)


def sum_kernel(
    bricks,
    capacity,
    slot_ref,
    p_ref,
    scale_ref,
    x_ref,
    dest_ref,
    rows_ref,
    map_ref,
    other_ref,
    mine_ref,
    weights,
    even,
    odd,
    slots,
    volume,
):
    g = pl.program_id(0)
    groups = pl.num_programs(0)
    blocks, owned, block = p_ref.shape
    segments = dest_ref.shape[0] // groups
    per_tile = TILE // 128
    tiles = segments // per_tile
    span = map_ref.shape[2]
    core = lax.rem(lax.axis_index("ori"), 2)

    @pl.when(g == 0)
    def _():
        zero = jnp.zeros((512, 128), jnp.float32)

        def clear(i, ignored):
            slots[pl.ds(pl.multiple_of(i * 512, 512), 512), :] = zero
            return ignored

        lax.fori_loop(0, slots.shape[0] // 512, clear, 0)
        volume[...] = jnp.zeros_like(volume)

    for k in range(blocks):
        weights[:, k * block : (k + 1) * block] = (p_ref[k] * scale_ref[k]).astype(jnp.bfloat16)

    def scatter(held, base):
        for s in range(per_tile):
            for r in range(owned // 8):
                values = held[r * 8 : r * 8 + 8, s * 128 : (s + 1) * 128]
                for k in range(8):
                    slot = slot_ref[base + s * owned + r * 8 + k]
                    slots[pl.ds(slot, 1), :] = values[k : k + 1, :]

    def product(t):
        columns = pl.ds(pl.multiple_of(t * TILE, TILE), TILE)
        return dot(weights[...], x_ref[:, columns])

    def pair(j, ignored):
        base = (g * segments + 2 * j * per_tile) * owned
        even[...] = product(2 * j)
        scatter(odd, base)
        odd[...] = product(2 * j + 1)
        scatter(even, base + per_tile * owned)
        return ignored

    lax.fori_loop(0, tiles // 2, pair, 0)

    ones = jnp.ones((8, blocks * block), jnp.bfloat16)
    sums = dot(ones, weights[...], NT)[0:1]
    high = sums.astype(jnp.bfloat16).astype(jnp.float32)
    low = sums - high

    def weigh(s, ignored):
        dest = dest_ref[g * segments + s]
        member = lax.broadcasted_iota(jnp.int32, (bricks, owned), 0) == dest
        parts = [jnp.where(member, part, 0.0).astype(jnp.bfloat16) for part in (high, low)]
        landed = one_hot_rows(BRICK_ROWS, rows_ref[g * segments + s])
        volume[...] += dot(parts[0], landed, NT) + dot(parts[1], landed, NT)
        return ignored

    lax.fori_loop(0, segments, weigh, 0)

    @pl.when(g == groups - 1)
    def _():
        scatter(odd, groups * segments * owned)
        sub = lax.broadcasted_iota(jnp.int32, (EXTRA_ROWS, 128), 0)

        def grid_brick(i, out_ref, parity):
            b = 2 * i + parity
            values = slots[pl.ds(pl.multiple_of(b * span, 8), span), :].astype(jnp.bfloat16)
            cells = dot(one_hot_rows(BRICK_ROWS, map_ref[b]), values)
            out_ref[i, 0:BRICK_ROWS, :] = cells.astype(jnp.bfloat16)
            total = volume[pl.ds(b, 1), :]
            top = total.astype(jnp.bfloat16).astype(jnp.float32)
            rest = total - top
            extra = jnp.where(sub == 0, top[:, :128], jnp.where(sub == 1, top[:, 128:], 0.0))
            extra += jnp.where(sub == 2, rest[:, :128], jnp.where(sub == 3, rest[:, 128:], 0.0))
            out_ref[i, BRICK_ROWS : BRICK_ROWS + EXTRA_ROWS, :] = extra.astype(jnp.bfloat16)

        def others(i, ignored):
            grid_brick(i, other_ref, 1 - core)
            return ignored

        def own(i, ignored):
            grid_brick(i, mine_ref, core)
            return ignored

        lax.fori_loop(0, bricks // 2, others, 0)
        lax.fori_loop(0, bricks // 2, own, 0)


def sum_step(bricks, groups, capacity, slot, p, scale, x, dest, rows, row_map):
    blocks, orients, block = p.shape
    width = x.shape[1]
    owned = orients // groups
    whole = lambda a: pl.BlockSpec(
        a.shape, lambda g: (0,) * a.ndim, pipeline_mode=pl.Buffered(1)
    )
    out = jax.ShapeDtypeStruct((bricks // 2, BRICK_ROWS + EXTRA_ROWS, 128), jnp.bfloat16)
    return pl.pallas_call(
        functools.partial(sum_kernel, bricks, capacity),
        grid=(groups,),
        out_shape=[out, out],
        in_specs=[
            SMEM,
            pl.BlockSpec((blocks, owned, block), lambda g: (0, g, 0)),
            whole(scale),
            whole(x),
            whole(dest),
            whole(rows),
            whole(row_map),
        ],
        out_specs=[whole(out), whole(out)],
        scratch_shapes=[
            pltpu.VMEM((owned, blocks * block), jnp.bfloat16),
            pltpu.VMEM((owned, TILE), jnp.float32),
            pltpu.VMEM((owned, TILE), jnp.float32),
            pltpu.VMEM((bricks * groups * capacity + 512, 128), jnp.float32),
            pltpu.VMEM((bricks, BRICK_ROWS), jnp.float32),
        ],
        compiler_params=pltpu.CompilerParams(vmem_limit_bytes=56 << 20),
        cost_estimate=pl.CostEstimate(
            flops=2 * blocks * block * orients * width, bytes_accessed=24 << 20, transcendentals=0
        ),
        name="sum_and_grid",
    )(slot, p, scale, x, dest, rows, row_map)


def body(images, projections, brick_dest, brick_rows, kernel):
    image_groups = lax.axis_size("img")
    orient_groups = lax.axis_size("ori")
    chips = orient_groups // 2
    bricks = image_groups * orient_groups
    orients, segments = brick_rows.shape
    owned = orients // image_groups
    capacity = max(2, 2 * owned * segments // bricks)
    me = lax.axis_index("ori")

    swap = [(i, i ^ 1) for i in range(orient_groups)]
    up = [(i, i + 2) for i in range(orient_groups - 2)]
    down = [(i + 2, i) for i in range(orient_groups - 2)]

    with jax.named_scope("place_segments"):

        def lanes(values):
            values = values.reshape(image_groups, owned, segments).transpose(0, 2, 1)
            return values.reshape(image_groups * segments, 1, owned)

        dest, rows = lanes(brick_dest), lanes(brick_rows)
        room = max(128, capacity)
        slot, row_map = pl.pallas_call(
            functools.partial(place_kernel, bricks, image_groups, capacity),
            out_shape=[
                jax.ShapeDtypeStruct(dest.shape, jnp.int32),
                jax.ShapeDtypeStruct((image_groups, bricks, room), jnp.int32),
            ],
            in_specs=[VMEM, VMEM],
            out_specs=[VMEM, VMEM],
            name="place_segments",
        )(dest, rows)
        row_map = row_map[:, :, :capacity].transpose(1, 0, 2).reshape(bricks, 1, image_groups * capacity)
        unused = jnp.full(((TILE // 128) * owned,), bricks * image_groups * capacity, jnp.int32)
        slot = jnp.concatenate([unused, slot.reshape(-1)])

    with jax.named_scope("score"):
        from_below = from_above = images
        carry = score_step(
            chips,
            ((0, False), (0, True)),
            (images, lax.ppermute(images, "ori", swap)),
            projections,
            None,
        )
        for distance in range(1, chips):
            from_below = lax.ppermute(from_below, "ori", up)
            from_above = lax.ppermute(from_above, "ori", down)
            arrived = (
                from_below,
                from_above,
                lax.ppermute(from_below, "ori", swap),
                lax.ppermute(from_above, "ori", swap),
            )
            candidates = (
                (-distance, False),
                (distance, False),
                (-distance, True),
                (distance, True),
            )
            carry = score_step(chips, candidates, arrived, projections, carry)
        _, p, x, stats = carry

    with jax.named_scope("softmax_total"):
        own_largest, own_total = stats[:, 0], stats[:, 1]
        pair = jnp.stack([own_largest, own_total])
        step = 1
        while step < orient_groups:
            partner = [(i, i ^ step) for i in range(orient_groups)]
            other = lax.ppermute(pair, "ori", partner)
            largest = jnp.maximum(pair[0], other[0])
            total = pair[1] * jnp.exp(pair[0] - largest) + other[1] * jnp.exp(other[0] - largest)
            pair = jnp.stack([largest, total])
            step *= 2
        scale = jnp.exp(own_largest - pair[0]) / pair[1]
        scale = scale[:, None, :]

    with jax.named_scope("sum_and_grid"):
        other_cells, cells = sum_step(
            bricks, image_groups, capacity, slot, p, scale, x, dest, rows, row_map
        )

    with jax.named_scope("brick_sums"):
        height = BRICK_ROWS + EXTRA_ROWS

        def add_up(cells, axis, ways, stride):
            own = lax.axis_index(axis) // stride
            total = lax.dynamic_index_in_dim(cells, own, 0, keepdims=False).astype(jnp.float32)
            for k in range(1, ways):
                perm = [(i, i ^ (k * stride)) for i in range(ways * stride)]
                part = lax.dynamic_index_in_dim(cells, own ^ k, 0, keepdims=False)
                total += lax.ppermute(part, axis, perm).astype(jnp.float32)
            return total

        other_cells = lax.ppermute(other_cells, "ori", swap)
        cells = cells.astype(jnp.float32) + other_cells.astype(jnp.float32)
        cells = cells.astype(jnp.bfloat16).reshape(image_groups, chips, height, 128)
        cells = add_up(cells, "img", image_groups, 1).astype(jnp.bfloat16)
        cells = add_up(cells, "ori", chips, 2)

    gridded = cells[:BRICK_ROWS]
    data_volume = jnp.dot(gridded, kernel[0].astype(jnp.float32), precision=lax.Precision.HIGHEST)
    extra = cells[BRICK_ROWS:]
    weight_volume = (extra[0:2] + extra[2:4]).reshape(1, BRICK_ROWS)
    return (data_volume[None], weight_volume)


def solution(mesh):
    placed = (
        P(("img", "ori"), None),
        P("ori", None),
        P("ori", None, None),
        P("ori", None),
        P(("img", "ori"), None, None),
    )
    return jax.shard_map(
        body,
        mesh=mesh,
        in_specs=placed,
        out_specs=(P(("img", "ori"), None, None), P(("img", "ori"), None)),
        check_vma=False,
    )
```

```python
import functools

import jax
import jax.numpy as jnp
from jax import lax
from jax.experimental import pallas as pl
from jax.experimental.pallas import tpu as pltpu
from jax.sharding import PartitionSpec as P

BRICK_ROWS = 256
EXTRA_ROWS = 16
TILE = 256
temper_scale = 4.0

ANY = pl.BlockSpec(memory_space=pl.ANY)
VMEM = pl.BlockSpec(memory_space=pltpu.VMEM)
SMEM = pl.BlockSpec(memory_space=pltpu.SMEM)
NN = (((1,), (0,)), ((), ()))
NT = (((1,), (1,)), ((), ()))


def dot(a, b, dims=NN):
    return lax.dot_general(a, b, dims, preferred_element_type=jnp.float32)


def one_hot_rows(count, row):
    numbers = lax.broadcasted_iota(jnp.int32, (count, row.shape[1]), 0)
    return jnp.where(numbers == row, 1.0, 0.0).astype(jnp.bfloat16)


def place_kernel(bricks, groups, capacity, dest_ref, rows_ref, slot_ref, map_ref):
    width = dest_ref.shape[2]
    segments = dest_ref.shape[0] // groups
    room = map_ref.shape[2]
    upper = (
        lax.broadcasted_iota(jnp.int32, (width, width), 0)
        <= lax.broadcasted_iota(jnp.int32, (width, width), 1)
    )
    upper = jnp.where(upper, 1.0, 0.0).astype(jnp.bfloat16)
    ones = jnp.ones((width, width), jnp.bfloat16)

    def group(g, ignored):
        dests = [dest_ref[g * segments + s] for s in range(segments)]
        members = [one_hot_rows(bricks, dest) for dest in dests]
        stacked = jnp.concatenate(members, axis=0)
        within = dot(stacked, upper)
        totals = dot(stacked, ones)
        taken = jnp.zeros((bricks, width), jnp.float32)
        marked, ranks = [], []
        for s in range(segments):
            part = slice(s * bricks, (s + 1) * bricks)
            member = members[s].astype(jnp.float32)
            rank = jnp.sum(member * (within[part] + taken), axis=0, keepdims=True) - 1.0
            rank = rank.astype(jnp.int32)
            taken += totals[part]
            slot_ref[g * segments + s] = (dests[s] * groups + g) * capacity + rank
            row = (rows_ref[g * segments + s] + 1).astype(jnp.float32)
            marked.append((member * row).astype(jnp.bfloat16))
            ranks.append(one_hot_rows(room, rank))
        row_map = dot(jnp.concatenate(marked, axis=1), jnp.concatenate(ranks, axis=1), NT)
        map_ref[g] = row_map.astype(jnp.int32) - 1
        return ignored

    lax.fori_loop(0, groups, group, 0)


def score_kernel(chips, candidates, first, *refs):
    n = len(candidates)
    images, refs = refs[:n], refs[n:]
    proj_ref, refs = refs[0], refs[1:]
    if not first:
        norm_in, refs = refs[0], refs[4:]
    if first:
        norm_ref, refs = refs[0], refs[1:]
    else:
        norm_ref = norm_in
    p_hbm, x_hbm, stat_hbm, held, p_buf, stat_buf, sem_in, sem_p, sem_x, sem_s = refs
    block = held.shape[1]
    orients = proj_ref.shape[0]
    chunk = min(256, orients)
    me = lax.axis_index("ori")
    chip, core = me // 2, lax.rem(me, 2)
    plan = []
    for shift, other in candidates:
        source = chip + shift
        valid = jnp.logical_and(source >= 0, source < chips)
        plan.append((valid, jnp.clip(source, 0, chips - 1) * 2 + (1 - core if other else core)))

    def copies(i):
        slot = plan[i][1]
        rows = pl.ds(pl.multiple_of(slot * block, block), block)
        return (
            lambda: pltpu.make_async_copy(images[i], held.at[i], sem_in.at[i]),
            lambda: pltpu.make_async_copy(held.at[i], x_hbm.at[rows], sem_x.at[i]),
            lambda: pltpu.make_async_copy(p_buf.at[i], p_hbm.at[slot], sem_p.at[i]),
            lambda: pltpu.make_async_copy(stat_buf.at[i], stat_hbm.at[slot], sem_s.at[i]),
        )

    for i in range(n):

        @pl.when(plan[i][0])
        def _(i=i):
            copies(i)[0]().start()

    if first:

        def square(r, ignored):
            rows = pl.ds(pl.multiple_of(r * chunk, chunk), chunk)
            values = proj_ref[rows, :].astype(jnp.float32)
            total = jnp.sum(values * values, axis=1, keepdims=True)
            norm_ref[rows, :] = jnp.broadcast_to(total, (chunk, norm_ref.shape[1]))
            return ignored

        lax.fori_loop(0, orients // chunk, square, 0)

    for i in range(n):

        @pl.when(plan[i][0])
        def _(i=i):
            fetch, keep, out, stats = copies(i)
            fetch().wait()
            keep().start()

            def score(r, largest):
                rows = pl.ds(pl.multiple_of(r * chunk, chunk), chunk)
                found = dot(proj_ref[rows, :], held[i], NT)
                norm = norm_ref[rows, 0:1]
                found = temper_scale * (found - 0.5 * norm)
                p_buf[i, rows, :] = found
                return jnp.maximum(largest, jnp.max(found, axis=0, keepdims=True))

            largest = lax.fori_loop(
                0, orients // chunk, score, jnp.full((1, block), -jnp.inf, jnp.float32)
            )

            def exponential(r, total):
                rows = pl.ds(pl.multiple_of(r * chunk, chunk), chunk)
                value = jnp.exp(p_buf[i, rows, :] - largest)
                p_buf[i, rows, :] = value
                return total + jnp.sum(value, axis=0, keepdims=True)

            total = lax.fori_loop(
                0, orients // chunk, exponential, jnp.zeros((1, block), jnp.float32)
            )
            out().start()
            pick = lax.broadcasted_iota(jnp.int32, (8, block), 0) == 0
            stat_buf[i] = jnp.where(pick, largest, total)
            stats().start()

    for i in range(n):

        @pl.when(plan[i][0])
        def _(i=i):
            for copy in copies(i)[1:]:
                copy().wait()


def score_step(chips, candidates, images, projections, carry):
    block, width = images[0].shape
    orients = projections.shape[0]
    blocks = 2 * chips
    n = len(images)
    first = carry is None
    shapes = [
        jax.ShapeDtypeStruct((blocks, orients, block), jnp.float32),
        jax.ShapeDtypeStruct((blocks * block, width), jnp.bfloat16),
        jax.ShapeDtypeStruct((blocks, 8, block), jnp.float32),
    ]
    in_specs = [ANY] * n + [VMEM]
    args = list(images) + [projections]
    if first:
        out_shape = [jax.ShapeDtypeStruct((orients, 128), jnp.float32)] + shapes
        out_specs = [VMEM] + [ANY] * 3
        aliases = {}
    else:
        in_specs += [VMEM] + [ANY] * 3
        args += list(carry)
        out_shape, out_specs = shapes, [ANY] * 3
        aliases = {n + 2 + k: k for k in range(3)}
    out = pl.pallas_call(
        functools.partial(score_kernel, chips, candidates, first),
        out_shape=out_shape,
        in_specs=in_specs,
        out_specs=out_specs,
        scratch_shapes=[
            pltpu.VMEM((n, block, width), jnp.bfloat16),
            pltpu.VMEM((n, orients, block), jnp.float32),
            pltpu.VMEM((n, 8, block), jnp.float32),
            pltpu.SemaphoreType.DMA((n,)),
            pltpu.SemaphoreType.DMA((n,)),
            pltpu.SemaphoreType.DMA((n,)),
            pltpu.SemaphoreType.DMA((n,)),
        ],
        input_output_aliases=aliases,
        compiler_params=pltpu.CompilerParams(vmem_limit_bytes=40 << 20),
        cost_estimate=pl.CostEstimate(
            flops=2 * n * block * orients * width, bytes_accessed=n * (4 << 20), transcendentals=0
        ),
        name="score_blocks",
    )(*args)
    return tuple(out) if first else (carry[0],) + tuple(out)


def sum_kernel(
    bricks,
    capacity,
    slot_ref,
    p_ref,
    scale_ref,
    x_ref,
    dest_ref,
    rows_ref,
    map_ref,
    other_ref,
    mine_ref,
    weights,
    even,
    odd,
    slots,
    volume,
):
    g = pl.program_id(0)
    groups = pl.num_programs(0)
    blocks, owned, block = p_ref.shape
    segments = dest_ref.shape[0] // groups
    per_tile = TILE // 128
    tiles = segments // per_tile
    span = map_ref.shape[2]
    core = lax.rem(lax.axis_index("ori"), 2)

    @pl.when(g == 0)
    def _():
        zero = jnp.zeros((512, 128), jnp.float32)

        def clear(i, ignored):
            slots[pl.ds(pl.multiple_of(i * 512, 512), 512), :] = zero
            return ignored

        lax.fori_loop(0, slots.shape[0] // 512, clear, 0)
        volume[...] = jnp.zeros_like(volume)

    for k in range(blocks):
        weights[:, k * block : (k + 1) * block] = (p_ref[k] * scale_ref[k]).astype(jnp.bfloat16)

    def scatter(held, base):
        for s in range(per_tile):
            for r in range(owned // 8):
                values = held[r * 8 : r * 8 + 8, s * 128 : (s + 1) * 128]
                for k in range(8):
                    slot = slot_ref[base + s * owned + r * 8 + k]
                    slots[pl.ds(slot, 1), :] = values[k : k + 1, :]

    def product(t):
        columns = pl.ds(pl.multiple_of(t * TILE, TILE), TILE)
        return dot(weights[...], x_ref[:, columns])

    ones = jnp.ones((8, blocks * block), jnp.bfloat16)
    sums = dot(ones, weights[...], NT)[0:1]
    high = sums.astype(jnp.bfloat16).astype(jnp.float32)
    low = sums - high

    def weigh(s):
        dest = dest_ref[g * segments + s]
        member = lax.broadcasted_iota(jnp.int32, (bricks, owned), 0) == dest
        parts = [jnp.where(member, part, 0.0).astype(jnp.bfloat16) for part in (high, low)]
        return jnp.concatenate(parts, axis=0), one_hot_rows(BRICK_ROWS, rows_ref[g * segments + s])

    def pair(j, ignored):
        both = [weigh(2 * j * per_tile + k) for k in range(2 * per_tile)]
        carried = jnp.concatenate([first for first, _ in both], axis=1)
        landed = jnp.concatenate([second for _, second in both], axis=1)
        volume[...] += dot(carried, landed, NT)
        base = (g * segments + 2 * j * per_tile) * owned
        even[...] = product(2 * j)
        scatter(odd, base)
        odd[...] = product(2 * j + 1)
        scatter(even, base + per_tile * owned)
        return ignored

    lax.fori_loop(0, tiles // 2, pair, 0)

    @pl.when(g == groups - 1)
    def _():
        scatter(odd, groups * segments * owned)
        sub = lax.broadcasted_iota(jnp.int32, (EXTRA_ROWS, 128), 0)
        unroll = 8

        def grid_brick(i, out_ref, parity):
            b = 2 * i + parity
            values = slots[pl.ds(pl.multiple_of(b * span, 8), span), :].astype(jnp.bfloat16)
            cells = dot(one_hot_rows(BRICK_ROWS, map_ref[b]), values)
            out_ref[i, 0:BRICK_ROWS, :] = cells.astype(jnp.bfloat16)
            total = volume[pl.ds(b, 1), :] + volume[pl.ds(bricks + b, 1), :]
            top = total.astype(jnp.bfloat16).astype(jnp.float32)
            rest = total - top
            extra = jnp.where(sub == 0, top[:, :128], jnp.where(sub == 1, top[:, 128:], 0.0))
            extra += jnp.where(sub == 2, rest[:, :128], jnp.where(sub == 3, rest[:, 128:], 0.0))
            out_ref[i, BRICK_ROWS : BRICK_ROWS + EXTRA_ROWS, :] = extra.astype(jnp.bfloat16)

        def others(i, ignored):
            for k in range(unroll):
                grid_brick(i * unroll + k, other_ref, 1 - core)
            return ignored

        def own(i, ignored):
            for k in range(unroll):
                grid_brick(i * unroll + k, mine_ref, core)
            return ignored

        lax.fori_loop(0, bricks // 2 // unroll, others, 0)
        lax.fori_loop(0, bricks // 2 // unroll, own, 0)


def sum_step(bricks, groups, capacity, slot, p, scale, x, dest, rows, row_map):
    blocks, orients, block = p.shape
    width = x.shape[1]
    owned = orients // groups
    whole = lambda a: pl.BlockSpec(
        a.shape, lambda g: (0,) * a.ndim, pipeline_mode=pl.Buffered(1)
    )
    out = jax.ShapeDtypeStruct((bricks // 2, BRICK_ROWS + EXTRA_ROWS, 128), jnp.bfloat16)
    return pl.pallas_call(
        functools.partial(sum_kernel, bricks, capacity),
        grid=(groups,),
        out_shape=[out, out],
        in_specs=[
            SMEM,
            pl.BlockSpec((blocks, owned, block), lambda g: (0, g, 0)),
            whole(scale),
            whole(x),
            whole(dest),
            whole(rows),
            whole(row_map),
        ],
        out_specs=[whole(out), whole(out)],
        scratch_shapes=[
            pltpu.VMEM((owned, blocks * block), jnp.bfloat16),
            pltpu.VMEM((owned, TILE), jnp.float32),
            pltpu.VMEM((owned, TILE), jnp.float32),
            pltpu.VMEM((bricks * groups * capacity + 512, 128), jnp.float32),
            pltpu.VMEM((2 * bricks, BRICK_ROWS), jnp.float32),
        ],
        compiler_params=pltpu.CompilerParams(vmem_limit_bytes=56 << 20),
        cost_estimate=pl.CostEstimate(
            flops=2 * blocks * block * orients * width, bytes_accessed=24 << 20, transcendentals=0
        ),
        name="sum_and_grid",
    )(slot, p, scale, x, dest, rows, row_map)


def body(images, projections, brick_dest, brick_rows, kernel):
    image_groups = lax.axis_size("img")
    orient_groups = lax.axis_size("ori")
    chips = orient_groups // 2
    bricks = image_groups * orient_groups
    orients, segments = brick_rows.shape
    owned = orients // image_groups
    capacity = max(2, 2 * owned * segments // bricks)
    me = lax.axis_index("ori")

    swap = [(i, i ^ 1) for i in range(orient_groups)]
    up = [(i, i + 2) for i in range(orient_groups - 2)]
    down = [(i + 2, i) for i in range(orient_groups - 2)]

    with jax.named_scope("place_segments"):

        def lanes(values):
            values = values.reshape(image_groups, owned, segments).transpose(0, 2, 1)
            return values.reshape(image_groups * segments, 1, owned)

        dest, rows = lanes(brick_dest), lanes(brick_rows)
        room = max(128, capacity)
        slot, row_map = pl.pallas_call(
            functools.partial(place_kernel, bricks, image_groups, capacity),
            out_shape=[
                jax.ShapeDtypeStruct(dest.shape, jnp.int32),
                jax.ShapeDtypeStruct((image_groups, bricks, room), jnp.int32),
            ],
            in_specs=[VMEM, VMEM],
            out_specs=[VMEM, VMEM],
            name="place_segments",
        )(dest, rows)
        row_map = row_map[:, :, :capacity].transpose(1, 0, 2).reshape(bricks, 1, image_groups * capacity)
        unused = jnp.full(((TILE // 128) * owned,), bricks * image_groups * capacity, jnp.int32)
        placed = (jnp.concatenate([unused, slot.reshape(-1)]), row_map, dest, rows)

    with jax.named_scope("score"):
        from_below = from_above = images
        carry = score_step(
            chips,
            ((0, False), (0, True)),
            (images, lax.ppermute(images, "ori", swap)),
            projections,
            None,
        )
        for distance in range(1, chips):
            from_below = lax.ppermute(from_below, "ori", up)
            from_above = lax.ppermute(from_above, "ori", down)
            from_below, from_above, carry, placed = lax.optimization_barrier(
                (from_below, from_above, carry, placed)
            )
            arrived = (
                from_below,
                from_above,
                lax.ppermute(from_below, "ori", swap),
                lax.ppermute(from_above, "ori", swap),
            )
            candidates = (
                (-distance, False),
                (distance, False),
                (-distance, True),
                (distance, True),
            )
            carry = score_step(chips, candidates, arrived, projections, carry)
        _, p, x, stats = carry
        slot, row_map, dest, rows = placed

    with jax.named_scope("softmax_total"):
        own_largest, own_total = stats[:, 0], stats[:, 1]
        pair = jnp.stack([own_largest, own_total])
        step = 1
        while step < orient_groups:
            partner = [(i, i ^ step) for i in range(orient_groups)]
            other = lax.ppermute(pair, "ori", partner)
            largest = jnp.maximum(pair[0], other[0])
            total = pair[1] * jnp.exp(pair[0] - largest) + other[1] * jnp.exp(other[0] - largest)
            pair = jnp.stack([largest, total])
            step *= 2
        scale = jnp.exp(own_largest - pair[0]) / pair[1]
        scale = scale[:, None, :]

    with jax.named_scope("sum_and_grid"):
        other_cells, cells = sum_step(
            bricks, image_groups, capacity, slot, p, scale, x, dest, rows, row_map
        )

    with jax.named_scope("brick_sums"):
        height = BRICK_ROWS + EXTRA_ROWS

        def add_up(cells, axis, ways, stride):
            own = lax.axis_index(axis) // stride
            total = lax.dynamic_index_in_dim(cells, own, 0, keepdims=False).astype(jnp.float32)
            for k in range(1, ways):
                perm = [(i, i ^ (k * stride)) for i in range(ways * stride)]
                part = lax.dynamic_index_in_dim(cells, own ^ k, 0, keepdims=False)
                total += lax.ppermute(part, axis, perm).astype(jnp.float32)
            return total

        other_cells = lax.ppermute(other_cells, "ori", swap)
        cells = cells.astype(jnp.float32) + other_cells.astype(jnp.float32)
        cells = cells.astype(jnp.bfloat16).reshape(image_groups, chips, height, 128)
        cells = add_up(cells, "img", image_groups, 1).astype(jnp.bfloat16)
        cells = add_up(cells, "ori", chips, 2)

    gridded = cells[:BRICK_ROWS]
    data_volume = jnp.dot(gridded, kernel[0].astype(jnp.float32), precision=lax.Precision.HIGHEST)
    extra = cells[BRICK_ROWS:]
    weight_volume = (extra[0:2] + extra[2:4]).reshape(1, BRICK_ROWS)
    return (data_volume[None], weight_volume)


def solution(mesh):
    placed = (
        P(("img", "ori"), None),
        P("ori", None),
        P("ori", None, None),
        P("ori", None),
        P(("img", "ori"), None, None),
    )
    return jax.shard_map(
        body,
        mesh=mesh,
        in_specs=placed,
        out_specs=(P(("img", "ori"), None, None), P(("img", "ori"), None)),
        check_vma=False,
    )
```

```python
import functools

import jax
import jax.numpy as jnp
from jax import lax
from jax.experimental import pallas as pl
from jax.experimental.pallas import tpu as pltpu
from jax.sharding import PartitionSpec as P

BRICK_ROWS = 256
EXTRA_ROWS = 16
TILE = 256
temper_scale = 4.0

ANY = pl.BlockSpec(memory_space=pl.ANY)
VMEM = pl.BlockSpec(memory_space=pltpu.VMEM)
SMEM = pl.BlockSpec(memory_space=pltpu.SMEM)
NN = (((1,), (0,)), ((), ()))
NT = (((1,), (1,)), ((), ()))


def dot(a, b, dims=NN):
    return lax.dot_general(a, b, dims, preferred_element_type=jnp.float32)


def one_hot_rows(count, row):
    numbers = lax.broadcasted_iota(jnp.int32, (count, row.shape[1]), 0).astype(jnp.bfloat16)
    one, zero = jnp.ones((), jnp.bfloat16), jnp.zeros((), jnp.bfloat16)
    return jnp.where(numbers == row.astype(jnp.bfloat16), one, zero)


def place_kernel(bricks, groups, capacity, dest_ref, rows_ref, slot_ref, map_ref):
    width = dest_ref.shape[2]
    segments = dest_ref.shape[0] // groups
    room = map_ref.shape[2]
    upper = (
        lax.broadcasted_iota(jnp.int32, (width, width), 0)
        <= lax.broadcasted_iota(jnp.int32, (width, width), 1)
    )
    upper = jnp.where(upper, 1.0, 0.0).astype(jnp.bfloat16)
    ones = jnp.ones((width, width), jnp.bfloat16)

    def group(g, ignored):
        dests = [dest_ref[g * segments + s] for s in range(segments)]
        members = [one_hot_rows(bricks, dest) for dest in dests]
        stacked = jnp.concatenate(members, axis=0)
        within = dot(stacked, upper)
        totals = dot(stacked, ones)
        taken = jnp.zeros((bricks, width), jnp.float32)
        marked, ranks = [], []
        for s in range(segments):
            part = slice(s * bricks, (s + 1) * bricks)
            member = members[s].astype(jnp.float32)
            rank = jnp.sum(member * (within[part] + taken), axis=0, keepdims=True) - 1.0
            rank = rank.astype(jnp.int32)
            taken += totals[part]
            slot_ref[g * segments + s] = (dests[s] * groups + g) * capacity + rank
            row = (rows_ref[g * segments + s] + 1).astype(jnp.float32)
            marked.append((member * row).astype(jnp.bfloat16))
            ranks.append(one_hot_rows(room, rank))
        row_map = dot(jnp.concatenate(marked, axis=1), jnp.concatenate(ranks, axis=1), NT)
        map_ref[g] = row_map.astype(jnp.int32) - 1
        return ignored

    lax.fori_loop(0, groups, group, 0)


def score_kernel(chips, candidates, first, *refs):
    n = len(candidates)
    images, refs = refs[:n], refs[n:]
    proj_ref, refs = refs[0], refs[1:]
    if not first:
        norm_in, refs = refs[0], refs[4:]
    if first:
        norm_ref, refs = refs[0], refs[1:]
    else:
        norm_ref = norm_in
    p_hbm, x_hbm, stat_hbm, held, p_buf, stat_buf, sem_in, sem_p, sem_x, sem_s = refs
    block = held.shape[1]
    orients = proj_ref.shape[0]
    chunk = min(512, orients)
    me = lax.axis_index("ori")
    chip, core = me // 2, lax.rem(me, 2)
    plan = []
    for distance, direct, own in candidates:
        below = (core == 0) if direct else (core == 1)
        source = chip + jnp.where(below, -distance, distance)
        valid = jnp.logical_and(source >= 0, source < chips)
        plan.append((valid, jnp.clip(source, 0, chips - 1) * 2 + (core if own else 1 - core)))

    def copies(i):
        slot = plan[i][1]
        rows = pl.ds(pl.multiple_of(slot * block, block), block)
        return (
            lambda: pltpu.make_async_copy(images[i], held.at[i], sem_in.at[i]),
            lambda: pltpu.make_async_copy(held.at[i], x_hbm.at[rows], sem_x.at[i]),
            lambda: pltpu.make_async_copy(p_buf.at[i], p_hbm.at[slot], sem_p.at[i]),
            lambda: pltpu.make_async_copy(stat_buf.at[i], stat_hbm.at[slot], sem_s.at[i]),
        )

    for i in range(n):

        @pl.when(plan[i][0])
        def _(i=i):
            copies(i)[0]().start()

    if first:

        def square(r, ignored):
            rows = pl.ds(pl.multiple_of(r * chunk, chunk), chunk)
            values = proj_ref[rows, :].astype(jnp.float32)
            total = jnp.sum(values * values, axis=1, keepdims=True)
            norm_ref[rows, :] = jnp.broadcast_to(total, (chunk, norm_ref.shape[1]))
            return ignored

        lax.fori_loop(0, orients // chunk, square, 0)

    for i in range(n):

        @pl.when(plan[i][0])
        def _(i=i):
            fetch, keep, out, stats = copies(i)
            fetch().wait()
            keep().start()

            def score(r, largest):
                rows = pl.ds(pl.multiple_of(r * chunk, chunk), chunk)
                found = dot(proj_ref[rows, :], held[i], NT)
                norm = norm_ref[rows, 0:1]
                found = temper_scale * (found - 0.5 * norm)
                p_buf[i, rows, :] = found
                return jnp.maximum(largest, jnp.max(found, axis=0, keepdims=True))

            largest = lax.fori_loop(
                0, orients // chunk, score, jnp.full((1, block), -jnp.inf, jnp.float32)
            )

            def exponential(r, total):
                rows = pl.ds(pl.multiple_of(r * chunk, chunk), chunk)
                value = jnp.exp(p_buf[i, rows, :] - largest)
                p_buf[i, rows, :] = value
                return total + jnp.sum(value, axis=0, keepdims=True)

            total = lax.fori_loop(
                0, orients // chunk, exponential, jnp.zeros((1, block), jnp.float32)
            )
            out().start()
            pick = lax.broadcasted_iota(jnp.int32, (8, block), 0) == 0
            stat_buf[i] = jnp.where(pick, largest, total)
            stats().start()

    for i in range(n):

        @pl.when(plan[i][0])
        def _(i=i):
            for copy in copies(i)[1:]:
                copy().wait()


def score_step(chips, candidates, images, projections, carry):
    block, width = images[0].shape
    orients = projections.shape[0]
    blocks = 2 * chips
    n = len(candidates)
    first = carry is None
    shapes = [
        jax.ShapeDtypeStruct((blocks, orients, block), jnp.float32),
        jax.ShapeDtypeStruct((blocks * block, width), jnp.bfloat16),
        jax.ShapeDtypeStruct((blocks, 8, block), jnp.float32),
    ]
    in_specs = [ANY] * n + [VMEM]
    args = list(images) + [projections]
    if first:
        out_shape = [jax.ShapeDtypeStruct((orients, 128), jnp.float32)] + shapes
        out_specs = [VMEM] + [ANY] * 3
        aliases = {}
    else:
        in_specs += [VMEM] + [ANY] * 3
        args += list(carry)
        out_shape, out_specs = shapes, [ANY] * 3
        aliases = {n + 2 + k: k for k in range(3)}
    out = pl.pallas_call(
        functools.partial(score_kernel, chips, candidates, first),
        out_shape=out_shape,
        in_specs=in_specs,
        out_specs=out_specs,
        scratch_shapes=[
            pltpu.VMEM((n, block, width), jnp.bfloat16),
            pltpu.VMEM((n, orients, block), jnp.float32),
            pltpu.VMEM((n, 8, block), jnp.float32),
            pltpu.SemaphoreType.DMA((n,)),
            pltpu.SemaphoreType.DMA((n,)),
            pltpu.SemaphoreType.DMA((n,)),
            pltpu.SemaphoreType.DMA((n,)),
        ],
        input_output_aliases=aliases,
        compiler_params=pltpu.CompilerParams(vmem_limit_bytes=20 << 20),
        cost_estimate=pl.CostEstimate(flops=1000, bytes_accessed=1000, transcendentals=0),
        name="score_blocks",
    )(*args)
    return tuple(out) if first else (carry[0],) + tuple(out)


def merge_kernel(a_ref, b_ref, out_ref):
    for k in range(a_ref.shape[0]):
        a, b = a_ref[k], b_ref[k]
        largest = jnp.maximum(a[0:1], b[0:1])
        total = a[1:2] * jnp.exp(a[0:1] - largest) + b[1:2] * jnp.exp(b[0:1] - largest)
        pick = lax.broadcasted_iota(jnp.int32, a.shape, 0) == 0
        out_ref[k] = jnp.where(pick, largest, total)


def merge_step(a, b):
    return pl.pallas_call(
        merge_kernel,
        out_shape=jax.ShapeDtypeStruct(a.shape, a.dtype),
        in_specs=[VMEM, VMEM],
        out_specs=VMEM,
        compiler_params=pltpu.CompilerParams(vmem_limit_bytes=4 << 20),
        cost_estimate=pl.CostEstimate(flops=1000, bytes_accessed=1000, transcendentals=0),
        name="merge_totals",
    )(a, b)


def sum_kernel(
    bricks,
    capacity,
    slot_ref,
    p_ref,
    stats_ref,
    totals_ref,
    x_ref,
    dest_ref,
    rows_ref,
    map_ref,
    other_ref,
    mine_ref,
    weights,
    even,
    odd,
    slots,
    volume,
):
    blocks, orients, block = p_ref.shape
    owned = dest_ref.shape[2]
    groups = orients // owned
    segments = dest_ref.shape[0] // groups
    per_tile = TILE // 128
    tiles = segments // per_tile
    span = map_ref.shape[2]
    core = lax.rem(lax.axis_index("ori"), 2)
    zero = jnp.zeros((512, 128), jnp.float32)

    def clear(i, ignored):
        slots[pl.ds(pl.multiple_of(i * 512, 512), 512), :] = zero
        return ignored

    lax.fori_loop(0, slots.shape[0] // 512, clear, 0)
    volume[...] = jnp.zeros_like(volume)

    def scatter(held, base):
        for s in range(per_tile):
            for r in range(owned // 8):
                values = held[r * 8 : r * 8 + 8, s * 128 : (s + 1) * 128]
                for k in range(8):
                    slot = slot_ref[base + s * owned + r * 8 + k]
                    slots[pl.ds(slot, 1), :] = values[k : k + 1, :]

    def product(t):
        columns = pl.ds(pl.multiple_of(t * TILE, TILE), TILE)
        return dot(weights[...], x_ref[:, columns])

    def group(g, ignored):
        rows = pl.ds(pl.multiple_of(g * owned, owned), owned)
        for k in range(blocks):
            scale = jnp.exp(stats_ref[k, 0:1] - totals_ref[k, 0:1]) / totals_ref[k, 1:2]
            weights[:, k * block : (k + 1) * block] = (p_ref[k, rows, :] * scale).astype(
                jnp.bfloat16
            )
        ones = jnp.ones((8, blocks * block), jnp.bfloat16)
        sums = dot(ones, weights[...], NT)[0:1]
        high = sums.astype(jnp.bfloat16).astype(jnp.float32)
        low = sums - high

        def weigh(s):
            dest = dest_ref[g * segments + s]
            member = lax.broadcasted_iota(jnp.int32, (bricks, owned), 0) == dest
            parts = [jnp.where(member, part, 0.0).astype(jnp.bfloat16) for part in (high, low)]
            landed = one_hot_rows(BRICK_ROWS, rows_ref[g * segments + s])
            return jnp.concatenate(parts, axis=0), landed

        def pair(j, ignored):
            both = [weigh(2 * j * per_tile + k) for k in range(2 * per_tile)]
            carried = jnp.concatenate([first for first, _ in both], axis=1)
            landed = jnp.concatenate([second for _, second in both], axis=1)
            volume[...] += dot(carried, landed, NT)
            base = (g * segments + 2 * j * per_tile) * owned
            even[...] = product(2 * j)
            scatter(odd, base)
            odd[...] = product(2 * j + 1)
            scatter(even, base + per_tile * owned)
            return ignored

        return lax.fori_loop(0, tiles // 2, pair, ignored)

    lax.fori_loop(0, groups, group, 0)
    scatter(odd, groups * segments * owned)
    sub = lax.broadcasted_iota(jnp.int32, (EXTRA_ROWS, 128), 0)
    unroll = 8

    def grid_brick(i, out_ref, parity):
        b = 2 * i + parity
        values = slots[pl.ds(pl.multiple_of(b * span, 8), span), :].astype(jnp.bfloat16)
        cells = dot(one_hot_rows(BRICK_ROWS, map_ref[b]), values)
        out_ref[i, 0:BRICK_ROWS, :] = cells.astype(out_ref.dtype)
        total = volume[pl.ds(b, 1), :] + volume[pl.ds(bricks + b, 1), :]
        top = total.astype(jnp.bfloat16).astype(jnp.float32)
        rest = total - top
        extra = jnp.where(sub == 0, top[:, :128], jnp.where(sub == 1, top[:, 128:], 0.0))
        extra += jnp.where(sub == 2, rest[:, :128], jnp.where(sub == 3, rest[:, 128:], 0.0))
        out_ref[i, BRICK_ROWS : BRICK_ROWS + EXTRA_ROWS, :] = extra.astype(out_ref.dtype)

    def others(i, ignored):
        for k in range(unroll):
            grid_brick(i * unroll + k, other_ref, 1 - core)
        return ignored

    def own(i, ignored):
        for k in range(unroll):
            grid_brick(i * unroll + k, mine_ref, core)
        return ignored

    lax.fori_loop(0, bricks // 2 // unroll, others, 0)
    lax.fori_loop(0, bricks // 2 // unroll, own, 0)


def sum_step(bricks, groups, capacity, slot, p, stats, totals, x, dest, rows, row_map):
    blocks, orients, block = p.shape
    width = x.shape[1]
    owned = orients // groups
    shape = (bricks // 2, BRICK_ROWS + EXTRA_ROWS, 128)
    return pl.pallas_call(
        functools.partial(sum_kernel, bricks, capacity),
        out_shape=[
            jax.ShapeDtypeStruct(shape, jnp.bfloat16),
            jax.ShapeDtypeStruct(shape, jnp.float32),
        ],
        in_specs=[SMEM] + [VMEM] * 7,
        out_specs=[VMEM, VMEM],
        scratch_shapes=[
            pltpu.VMEM((owned, blocks * block), jnp.bfloat16),
            pltpu.VMEM((owned, TILE), jnp.float32),
            pltpu.VMEM((owned, TILE), jnp.float32),
            pltpu.VMEM((bricks * groups * capacity + 512, 128), jnp.float32),
            pltpu.VMEM((2 * bricks, BRICK_ROWS), jnp.float32),
        ],
        compiler_params=pltpu.CompilerParams(vmem_limit_bytes=22 << 20),
        cost_estimate=pl.CostEstimate(
            flops=2 * blocks * block * orients * width, bytes_accessed=24 << 20, transcendentals=0
        ),
        name="sum_and_grid",
    )(slot, p, stats, totals, x, dest, rows, row_map)


def body(images, projections, brick_dest, brick_rows, kernel):
    image_groups = lax.axis_size("img")
    orient_groups = lax.axis_size("ori")
    chips = orient_groups // 2
    bricks = image_groups * orient_groups
    orients, segments = brick_rows.shape
    owned = orients // image_groups
    capacity = max(2, 2 * owned * segments // bricks)
    me = lax.axis_index("ori")

    swap = [(i, i ^ 1) for i in range(orient_groups)]
    along = [(i, i + 2) for i in range(0, orient_groups - 2, 2)]
    along += [(i + 2, i) for i in range(1, orient_groups - 2, 2)]

    with jax.named_scope("place_segments"):

        def lanes(values):
            values = values.reshape(image_groups, owned, segments).transpose(0, 2, 1)
            return values.reshape(image_groups * segments, 1, owned)

        dest, rows = lanes(brick_dest), lanes(brick_rows)
        room = max(128, capacity)
        slot, row_map = pl.pallas_call(
            functools.partial(place_kernel, bricks, image_groups, capacity),
            out_shape=[
                jax.ShapeDtypeStruct(dest.shape, jnp.int32),
                jax.ShapeDtypeStruct((image_groups, bricks, room), jnp.int32),
            ],
            in_specs=[VMEM, VMEM],
            out_specs=[VMEM, VMEM],
            compiler_params=pltpu.CompilerParams(vmem_limit_bytes=12 << 20),
            cost_estimate=pl.CostEstimate(flops=1000, bytes_accessed=1000, transcendentals=0),
            name="place_segments",
        )(dest, rows)
        row_map = row_map[:, :, :capacity].transpose(1, 0, 2).reshape(bricks, 1, image_groups * capacity)
        unused = jnp.full(((TILE // 128) * owned,), bricks * image_groups * capacity, jnp.int32)
        placed = (jnp.concatenate([unused, slot.reshape(-1)]), row_map, dest, rows)

    with jax.named_scope("score"):
        mate = lax.ppermute(images, "ori", swap)
        moving = [images, mate]
        mate, placed = lax.optimization_barrier((mate, placed))
        carry = score_step(
            chips, ((0, True, True), (0, True, False)), (images, mate), projections, None
        )

        def arrive(distance, q, part):
            own = q == 0
            both = (part, lax.ppermute(part, "ori", swap))
            return ((distance, True, own), (distance, False, not own)), both

        def score(waiting, carry):
            return score_step(chips, waiting[0], waiting[1], projections, carry)

        waiting = []
        for distance in range(1, chips):
            moving = [lax.ppermute(part, "ori", along) for part in moving]
            for q in range(2):
                if distance == 1:
                    if q == 0:
                        moving, carry = lax.optimization_barrier((moving, carry))
                elif distance == 2 and q == 0:
                    moving[q], carry = lax.optimization_barrier((moving[q], carry))
                else:
                    carry = score(waiting.pop(0), carry)
                    moving[q], carry = lax.optimization_barrier((moving[q], carry))
                waiting.append(arrive(distance, q, moving[q]))
        late = [sum(parts, ()) for parts in zip(*waiting)]
        carry = score(late, carry)
        _, p, x, stats = carry
        slot, row_map, dest, rows = placed

    with jax.named_scope("softmax_total"):
        totals = stats
        step = 1
        while step < orient_groups:
            partner = [(i, i ^ step) for i in range(orient_groups)]
            totals = merge_step(totals, lax.ppermute(totals, "ori", partner))
            step *= 2

    with jax.named_scope("sum_and_grid"):
        other_cells, cells = sum_step(
            bricks, image_groups, capacity, slot, p, stats, totals, x, dest, rows, row_map
        )

    with jax.named_scope("brick_sums"):
        height = BRICK_ROWS + EXTRA_ROWS

        def add_up(cells, axis, ways, stride):
            own = lax.axis_index(axis) // stride
            total = lax.dynamic_index_in_dim(cells, own, 0, keepdims=False).astype(jnp.float32)
            for k in range(1, ways):
                perm = [(i, i ^ (k * stride)) for i in range(ways * stride)]
                part = lax.dynamic_index_in_dim(cells, own ^ k, 0, keepdims=False)
                total += lax.ppermute(part, axis, perm).astype(jnp.float32)
            return total

        other_cells = lax.ppermute(other_cells, "ori", swap)
        cells = cells.astype(jnp.float32) + other_cells.astype(jnp.float32)
        cells = cells.astype(jnp.bfloat16).reshape(image_groups, chips, height, 128)
        cells = add_up(cells, "img", image_groups, 1).astype(jnp.bfloat16)
        cells = add_up(cells, "ori", chips, 2)

    gridded = cells[:BRICK_ROWS]
    data_volume = jnp.dot(gridded, kernel[0].astype(jnp.float32), precision=lax.Precision.HIGHEST)
    extra = cells[BRICK_ROWS:]
    weight_volume = (extra[0:2] + extra[2:4]).reshape(1, BRICK_ROWS)
    return (data_volume[None], weight_volume)


def solution(mesh):
    placed = (
        P(("img", "ori"), None),
        P("ori", None),
        P("ori", None, None),
        P("ori", None),
        P(("img", "ori"), None, None),
    )
    return jax.shard_map(
        body,
        mesh=mesh,
        in_specs=placed,
        out_specs=(P(("img", "ori"), None, None), P(("img", "ori"), None)),
        check_vma=False,
    )
```

```python
import functools

import jax
import jax.numpy as jnp
from jax import lax
from jax.experimental import pallas as pl
from jax.experimental.pallas import tpu as pltpu
from jax.sharding import PartitionSpec as P

BRICK_ROWS = 256
EXTRA_ROWS = 16
TILE = 256
temper_scale = 4.0

ANY = pl.BlockSpec(memory_space=pl.ANY)
VMEM = pl.BlockSpec(memory_space=pltpu.VMEM)
SMEM = pl.BlockSpec(memory_space=pltpu.SMEM)
NN = (((1,), (0,)), ((), ()))
NT = (((1,), (1,)), ((), ()))


def dot(a, b, dims=NN):
    return lax.dot_general(a, b, dims, preferred_element_type=jnp.float32)


def one_hot_rows(count, row):
    numbers = lax.broadcasted_iota(jnp.int32, (count, row.shape[1]), 0).astype(jnp.bfloat16)
    one, zero = jnp.ones((), jnp.bfloat16), jnp.zeros((), jnp.bfloat16)
    return jnp.where(numbers == row.astype(jnp.bfloat16), one, zero)


def place_kernel(bricks, groups, capacity, dest_ref, rows_ref, slot_ref, map_ref):
    width = dest_ref.shape[2]
    segments = dest_ref.shape[0] // groups
    room = map_ref.shape[2]
    upper = (
        lax.broadcasted_iota(jnp.int32, (width, width), 0)
        <= lax.broadcasted_iota(jnp.int32, (width, width), 1)
    )
    upper = jnp.where(upper, 1.0, 0.0).astype(jnp.bfloat16)
    ones = jnp.ones((width, width), jnp.bfloat16)

    def group(g, ignored):
        dests = [dest_ref[g * segments + s] for s in range(segments)]
        members = [one_hot_rows(bricks, dest) for dest in dests]
        stacked = jnp.concatenate(members, axis=0)
        within = dot(stacked, upper)
        totals = dot(stacked, ones)
        taken = jnp.zeros((bricks, width), jnp.float32)
        marked, ranks = [], []
        for s in range(segments):
            part = slice(s * bricks, (s + 1) * bricks)
            member = members[s].astype(jnp.float32)
            rank = jnp.sum(member * (within[part] + taken), axis=0, keepdims=True) - 1.0
            rank = rank.astype(jnp.int32)
            taken += totals[part]
            slot_ref[g * segments + s] = (dests[s] * groups + g) * capacity + rank
            row = (rows_ref[g * segments + s] + 1).astype(jnp.float32)
            marked.append((member * row).astype(jnp.bfloat16))
            ranks.append(one_hot_rows(room, rank))
        row_map = dot(jnp.concatenate(marked, axis=1), jnp.concatenate(ranks, axis=1), NT)
        map_ref[g] = row_map.astype(jnp.int32) - 1
        return ignored

    lax.fori_loop(0, groups, group, 0)


def score_kernel(chips, candidates, first, *refs):
    n = len(candidates)
    images, refs = refs[:n], refs[n:]
    proj_ref, refs = refs[0], refs[1:]
    if not first:
        norm_in, refs = refs[0], refs[4:]
    if first:
        norm_ref, refs = refs[0], refs[1:]
    else:
        norm_ref = norm_in
    p_hbm, x_hbm, stat_hbm, held, p_buf, stat_buf, sem_in, sem_p, sem_x, sem_s = refs
    block = held.shape[1]
    orients = proj_ref.shape[0]
    chunk = min(512, orients)
    me = lax.axis_index("ori")
    chip, core = me // 2, lax.rem(me, 2)
    plan = []
    for distance, direct, own in candidates:
        below = (core == 0) if direct else (core == 1)
        source = chip + jnp.where(below, -distance, distance)
        valid = jnp.logical_and(source >= 0, source < chips)
        plan.append((valid, jnp.clip(source, 0, chips - 1) * 2 + (core if own else 1 - core)))

    def copies(i):
        slot = plan[i][1]
        rows = pl.ds(pl.multiple_of(slot * block, block), block)
        return (
            lambda: pltpu.make_async_copy(images[i], held.at[i], sem_in.at[i]),
            lambda: pltpu.make_async_copy(held.at[i], x_hbm.at[rows], sem_x.at[i]),
            lambda: pltpu.make_async_copy(p_buf.at[i], p_hbm.at[slot], sem_p.at[i]),
            lambda: pltpu.make_async_copy(stat_buf.at[i], stat_hbm.at[slot], sem_s.at[i]),
        )

    for i in range(n):

        @pl.when(plan[i][0])
        def _(i=i):
            copies(i)[0]().start()

    if first:

        def square(r, ignored):
            rows = pl.ds(pl.multiple_of(r * chunk, chunk), chunk)
            values = proj_ref[rows, :].astype(jnp.float32)
            total = jnp.sum(values * values, axis=1, keepdims=True)
            norm_ref[rows, :] = jnp.broadcast_to(total, (chunk, norm_ref.shape[1]))
            return ignored

        lax.fori_loop(0, orients // chunk, square, 0)

    for i in range(n):

        @pl.when(plan[i][0])
        def _(i=i):
            fetch, keep, out, stats = copies(i)
            fetch().wait()
            keep().start()

            def score(r, largest):
                rows = pl.ds(pl.multiple_of(r * chunk, chunk), chunk)
                found = dot(proj_ref[rows, :], held[i], NT)
                norm = norm_ref[rows, 0:1]
                found = temper_scale * (found - 0.5 * norm)
                p_buf[i, rows, :] = found
                return jnp.maximum(largest, jnp.max(found, axis=0, keepdims=True))

            largest = lax.fori_loop(
                0, orients // chunk, score, jnp.full((1, block), -jnp.inf, jnp.float32)
            )

            def exponential(r, total):
                rows = pl.ds(pl.multiple_of(r * chunk, chunk), chunk)
                value = jnp.exp(p_buf[i, rows, :] - largest)
                p_buf[i, rows, :] = value
                return total + jnp.sum(value, axis=0, keepdims=True)

            total = lax.fori_loop(
                0, orients // chunk, exponential, jnp.zeros((1, block), jnp.float32)
            )
            out().start()
            pick = lax.broadcasted_iota(jnp.int32, (8, block), 0) == 0
            stat_buf[i] = jnp.where(pick, largest, total)
            stats().start()

    for i in range(n):

        @pl.when(plan[i][0])
        def _(i=i):
            for copy in copies(i)[1:]:
                copy().wait()


def score_step(chips, candidates, images, projections, carry):
    block, width = images[0].shape
    orients = projections.shape[0]
    blocks = 2 * chips
    n = len(candidates)
    first = carry is None
    shapes = [
        jax.ShapeDtypeStruct((blocks, orients, block), jnp.float32),
        jax.ShapeDtypeStruct((blocks * block, width), jnp.bfloat16),
        jax.ShapeDtypeStruct((blocks, 8, block), jnp.float32),
    ]
    in_specs = [ANY] * n + [VMEM]
    args = list(images) + [projections]
    if first:
        out_shape = [jax.ShapeDtypeStruct((orients, 128), jnp.float32)] + shapes
        out_specs = [VMEM] + [ANY] * 3
        aliases = {}
    else:
        in_specs += [VMEM] + [ANY] * 3
        args += list(carry)
        out_shape, out_specs = shapes, [ANY] * 3
        aliases = {n + 2 + k: k for k in range(3)}
    out = pl.pallas_call(
        functools.partial(score_kernel, chips, candidates, first),
        out_shape=out_shape,
        in_specs=in_specs,
        out_specs=out_specs,
        scratch_shapes=[
            pltpu.VMEM((n, block, width), jnp.bfloat16),
            pltpu.VMEM((n, orients, block), jnp.float32),
            pltpu.VMEM((n, 8, block), jnp.float32),
            pltpu.SemaphoreType.DMA((n,)),
            pltpu.SemaphoreType.DMA((n,)),
            pltpu.SemaphoreType.DMA((n,)),
            pltpu.SemaphoreType.DMA((n,)),
        ],
        input_output_aliases=aliases,
        compiler_params=pltpu.CompilerParams(vmem_limit_bytes=14 << 20),
        cost_estimate=pl.CostEstimate(flops=1000, bytes_accessed=1000, transcendentals=0),
        name="score_blocks",
    )(*args)
    return tuple(out) if first else (carry[0],) + tuple(out)


def merge_kernel(*refs):
    out_ref = refs[-1]
    for k in range(out_ref.shape[0]):
        sets = [ref[k] for ref in refs[:-1]]
        largest = functools.reduce(jnp.maximum, [a[0:1] for a in sets])
        total = sum(a[1:2] * jnp.exp(a[0:1] - largest) for a in sets)
        pick = lax.broadcasted_iota(jnp.int32, sets[0].shape, 0) == 0
        out_ref[k] = jnp.where(pick, largest, total)


def merge_step(*sets):
    return pl.pallas_call(
        merge_kernel,
        out_shape=jax.ShapeDtypeStruct(sets[0].shape, sets[0].dtype),
        in_specs=[VMEM] * len(sets),
        out_specs=VMEM,
        compiler_params=pltpu.CompilerParams(vmem_limit_bytes=4 << 20),
        cost_estimate=pl.CostEstimate(flops=1000, bytes_accessed=1000, transcendentals=0),
        name="merge_totals",
    )(*sets)


def sum_kernel(
    bricks,
    capacity,
    slot_ref,
    p_ref,
    stats_ref,
    totals_ref,
    x_ref,
    dest_ref,
    rows_ref,
    map_ref,
    other_ref,
    mine_ref,
    volume,
    weights,
    even,
    odd,
    slots,
):
    blocks, orients, block = p_ref.shape
    owned = dest_ref.shape[2]
    groups = orients // owned
    segments = dest_ref.shape[0] // groups
    per_tile = TILE // 128
    tiles = segments // per_tile
    core = lax.rem(lax.axis_index("ori"), 2)
    zero = jnp.zeros((512, 128), jnp.float32)

    def clear(i, ignored):
        slots[pl.ds(pl.multiple_of(i * 512, 512), 512), :] = zero
        return ignored

    lax.fori_loop(0, slots.shape[0] // 512, clear, 0)
    volume[...] = jnp.zeros_like(volume)

    def scatter(held, base):
        for s in range(per_tile):
            for r in range(owned // 8):
                values = held[r * 8 : r * 8 + 8, s * 128 : (s + 1) * 128]
                for k in range(8):
                    slot = slot_ref[base + s * owned + r * 8 + k]
                    slots[pl.ds(slot, 1), :] = values[k : k + 1, :]

    def product(t):
        columns = pl.ds(pl.multiple_of(t * TILE, TILE), TILE)
        return dot(weights[...], x_ref[:, columns])

    def group(g, ignored):
        rows = pl.ds(pl.multiple_of(g * owned, owned), owned)
        for k in range(blocks):
            scale = jnp.exp(stats_ref[k, 0:1] - totals_ref[k, 0:1]) / totals_ref[k, 1:2]
            weights[:, k * block : (k + 1) * block] = (p_ref[k, rows, :] * scale).astype(
                jnp.bfloat16
            )
        ones = jnp.ones((8, blocks * block), jnp.bfloat16)
        sums = dot(ones, weights[...], NT)[0:1]
        high = sums.astype(jnp.bfloat16).astype(jnp.float32)
        low = sums - high

        def weigh(s):
            dest = dest_ref[g * segments + s]
            member = lax.broadcasted_iota(jnp.int32, (bricks, owned), 0) == dest
            parts = [jnp.where(member, part, 0.0).astype(jnp.bfloat16) for part in (high, low)]
            landed = one_hot_rows(BRICK_ROWS, rows_ref[g * segments + s])
            return jnp.concatenate(parts, axis=0), landed

        def pair(j, ignored):
            both = [weigh(2 * j * per_tile + k) for k in range(2 * per_tile)]
            carried = jnp.concatenate([first for first, _ in both], axis=1)
            landed = jnp.concatenate([second for _, second in both], axis=1)
            volume[...] += dot(carried, landed, NT)
            base = (g * segments + 2 * j * per_tile) * owned
            even[...] = product(2 * j)
            scatter(odd, base)
            odd[...] = product(2 * j + 1)
            scatter(even, base + per_tile * owned)
            return ignored

        return lax.fori_loop(0, tiles // 2, pair, ignored)

    lax.fori_loop(0, groups, group, 0)
    scatter(odd, groups * segments * owned)
    span = map_ref.shape[2]

    def slots_of(i, parity):
        start = pl.multiple_of(brick_of(i, parity) * span, 8)
        return slots[pl.ds(start, span), :].astype(jnp.bfloat16)

    def keep(i, ignored):
        mine_ref[i] = slots_of(i, core)
        return ignored

    lax.fori_loop(0, bricks // 2, keep, 0)
    grid_bricks(1 - core, lambda i: slots_of(i, 1 - core), volume, map_ref, other_ref)


def brick_of(i, parity):
    chips = lax.axis_size("ori") // 2
    group = lax.bitwise_xor(lax.axis_index("img"), i // chips)
    chip = lax.bitwise_xor(lax.axis_index("ori") // 2, lax.rem(i, chips))
    return (group * chips + chip) * 2 + parity


def grid_bricks(parity, slots_of, volume, map_ref, out_ref):
    bricks = map_ref.shape[0]
    unroll = 8
    sub = lax.broadcasted_iota(jnp.int32, (EXTRA_ROWS, 128), 0)

    def grid_brick(i):
        b = brick_of(i, parity)
        cells = dot(one_hot_rows(BRICK_ROWS, map_ref[b]), slots_of(i))
        out_ref[i, 0:BRICK_ROWS, :] = cells.astype(out_ref.dtype)
        total = volume[pl.ds(b, 1), :] + volume[pl.ds(bricks + b, 1), :]
        top = total.astype(jnp.bfloat16).astype(jnp.float32)
        rest = total - top
        extra = jnp.where(sub == 0, top[:, :128], jnp.where(sub == 1, top[:, 128:], 0.0))
        extra += jnp.where(sub == 2, rest[:, :128], jnp.where(sub == 3, rest[:, 128:], 0.0))
        out_ref[i, BRICK_ROWS : BRICK_ROWS + EXTRA_ROWS, :] = extra.astype(out_ref.dtype)

    def step(i, ignored):
        for k in range(unroll):
            grid_brick(i * unroll + k)
        return ignored

    lax.fori_loop(0, bricks // 2 // unroll, step, 0)


def grid_kernel(slots, volume, map_ref, out_ref):
    core = lax.rem(lax.axis_index("ori"), 2)
    grid_bricks(core, lambda i: slots[i], volume, map_ref, out_ref)


def grid_step(slots, volume, row_map):
    bricks = row_map.shape[0]
    shape = (bricks // 2, BRICK_ROWS + EXTRA_ROWS, 128)
    return pl.pallas_call(
        grid_kernel,
        out_shape=jax.ShapeDtypeStruct(shape, jnp.float32),
        in_specs=[VMEM] * 3,
        out_specs=VMEM,
        compiler_params=pltpu.CompilerParams(vmem_limit_bytes=8 << 20),
        cost_estimate=pl.CostEstimate(flops=1000, bytes_accessed=1000, transcendentals=0),
        name="grid_own_bricks",
    )(slots, volume, row_map)


def sum_step(bricks, groups, capacity, slot, p, stats, totals, x, dest, rows, row_map):
    blocks, orients, block = p.shape
    width = x.shape[1]
    owned = orients // groups
    shape = (bricks // 2, BRICK_ROWS + EXTRA_ROWS, 128)
    return pl.pallas_call(
        functools.partial(sum_kernel, bricks, capacity),
        out_shape=[
            jax.ShapeDtypeStruct(shape, jnp.bfloat16),
            jax.ShapeDtypeStruct((bricks // 2, groups * capacity, 128), jnp.bfloat16),
            jax.ShapeDtypeStruct((2 * bricks, BRICK_ROWS), jnp.float32),
        ],
        in_specs=[SMEM] + [VMEM] * 7,
        out_specs=[VMEM] * 3,
        scratch_shapes=[
            pltpu.VMEM((owned, blocks * block), jnp.bfloat16),
            pltpu.VMEM((owned, TILE), jnp.float32),
            pltpu.VMEM((owned, TILE), jnp.float32),
            pltpu.VMEM((bricks * groups * capacity + 512, 128), jnp.float32),
        ],
        compiler_params=pltpu.CompilerParams(vmem_limit_bytes=19 << 20),
        cost_estimate=pl.CostEstimate(
            flops=2 * blocks * block * orients * width, bytes_accessed=24 << 20, transcendentals=0
        ),
        name="sum_and_grid",
    )(slot, p, stats, totals, x, dest, rows, row_map)


def body(images, projections, brick_dest, brick_rows, kernel):
    image_groups = lax.axis_size("img")
    orient_groups = lax.axis_size("ori")
    chips = orient_groups // 2
    bricks = image_groups * orient_groups
    orients, segments = brick_rows.shape
    owned = orients // image_groups
    capacity = max(2, 2 * owned * segments // bricks)
    me = lax.axis_index("ori")

    swap = [(i, i ^ 1) for i in range(orient_groups)]
    along = [(i, i + 2) for i in range(0, orient_groups - 2, 2)]
    along += [(i + 2, i) for i in range(1, orient_groups - 2, 2)]

    with jax.named_scope("place_segments"):

        def lanes(values):
            values = values.reshape(image_groups, owned, segments).transpose(0, 2, 1)
            return values.reshape(image_groups * segments, 1, owned)

        dest, rows = lanes(brick_dest), lanes(brick_rows)
        room = max(128, capacity)
        slot, row_map = pl.pallas_call(
            functools.partial(place_kernel, bricks, image_groups, capacity),
            out_shape=[
                jax.ShapeDtypeStruct(dest.shape, jnp.int32),
                jax.ShapeDtypeStruct((image_groups, bricks, room), jnp.int32),
            ],
            in_specs=[VMEM, VMEM],
            out_specs=[VMEM, VMEM],
            compiler_params=pltpu.CompilerParams(vmem_limit_bytes=8 << 20),
            cost_estimate=pl.CostEstimate(flops=1000, bytes_accessed=1000, transcendentals=0),
            name="place_segments",
        )(dest, rows)
        row_map = row_map[:, :, :capacity].transpose(1, 0, 2).reshape(bricks, 1, image_groups * capacity)
        unused = jnp.full(((TILE // 128) * owned,), bricks * image_groups * capacity, jnp.int32)
        placed = (jnp.concatenate([unused, slot.reshape(-1)]), row_map, dest, rows)

    with jax.named_scope("score"):
        mate = lax.ppermute(images, "ori", swap)
        moving = [images, mate]
        mate, placed = lax.optimization_barrier((mate, placed))
        carry = score_step(
            chips, ((0, True, True), (0, True, False)), (images, mate), projections, None
        )

        def arrive(distance, q, part):
            own = q == 0
            both = (part, lax.ppermute(part, "ori", swap))
            return ((distance, True, own), (distance, False, not own)), both

        def score(waiting, carry):
            return score_step(chips, waiting[0], waiting[1], projections, carry)

        waiting = []
        for distance in range(1, chips):
            moving = [lax.ppermute(part, "ori", along) for part in moving]
            for q in range(2):
                if distance == 1:
                    if q == 0:
                        moving, carry = lax.optimization_barrier((moving, carry))
                elif distance == 2 and q == 0:
                    moving[q], carry = lax.optimization_barrier((moving[q], carry))
                else:
                    carry = score(waiting.pop(0), carry)
                    if distance == chips - 1 and q == 1:
                        carry = score(waiting.pop(0), carry)
                    moving[q], carry = lax.optimization_barrier((moving[q], carry))
                waiting.append(arrive(distance, q, moving[q]))
        late = [sum(parts, ()) for parts in zip(*waiting)]
        carry = score(late, carry)
        _, p, x, stats = carry
        slot, row_map, dest, rows = placed

    with jax.named_scope("softmax_total"):
        totals = merge_step(stats, lax.ppermute(stats, "ori", swap))
        others = [
            lax.ppermute(totals, "ori", [(i, i ^ (2 * k)) for i in range(orient_groups)])
            for k in range(1, chips)
        ]
        totals = merge_step(totals, *others)

    with jax.named_scope("sum_and_grid"):
        other_cells, slots, volume = sum_step(
            bricks, image_groups, capacity, slot, p, stats, totals, x, dest, rows, row_map
        )

    with jax.named_scope("brick_sums"):
        height = BRICK_ROWS + EXTRA_ROWS

        def add_up(cells, axis, ways, stride):
            total = cells[0].astype(jnp.float32)
            for k in range(1, ways):
                perm = [(i, i ^ (k * stride)) for i in range(ways * stride)]
                part = cells[k].astype(jnp.bfloat16)
                total += lax.ppermute(part, axis, perm).astype(jnp.float32)
            return total

        other_cells = lax.ppermute(other_cells, "ori", swap)
        cells = grid_step(slots, volume, row_map)
        cells = cells + other_cells.astype(jnp.float32)
        cells = cells.reshape(image_groups, chips, height, 128)
        cells = add_up(cells, "img", image_groups, 1)
        cells = add_up(cells, "ori", chips, 2)

    gridded = cells[:BRICK_ROWS]
    data_volume = jnp.dot(gridded, kernel[0].astype(jnp.float32), precision=lax.Precision.HIGHEST)
    extra = cells[BRICK_ROWS:]
    weight_volume = (extra[0:2] + extra[2:4]).reshape(1, BRICK_ROWS)
    return (data_volume[None], weight_volume)


def solution(mesh):
    placed = (
        P(("img", "ori"), None),
        P("ori", None),
        P("ori", None, None),
        P("ori", None),
        P(("img", "ori"), None, None),
    )
    return jax.shard_map(
        body,
        mesh=mesh,
        in_specs=placed,
        out_specs=(P(("img", "ori"), None, None), P(("img", "ori"), None)),
        check_vma=False,
    )
```

```python
import functools

import jax
import jax.numpy as jnp
from jax import lax
from jax.experimental import pallas as pl
from jax.experimental.pallas import tpu as pltpu
from jax.sharding import PartitionSpec as P

BRICK_ROWS = 256
EXTRA_ROWS = 16
TILE = 256
temper_scale = 4.0

ANY = pl.BlockSpec(memory_space=pl.ANY)
VMEM = pl.BlockSpec(memory_space=pltpu.VMEM)
SMEM = pl.BlockSpec(memory_space=pltpu.SMEM)
NN = (((1,), (0,)), ((), ()))
NT = (((1,), (1,)), ((), ()))


def dot(a, b, dims=NN):
    return lax.dot_general(a, b, dims, preferred_element_type=jnp.float32)


def one_hot_rows(count, row):
    numbers = lax.broadcasted_iota(jnp.int32, (count, row.shape[1]), 0).astype(jnp.bfloat16)
    one, zero = jnp.ones((), jnp.bfloat16), jnp.zeros((), jnp.bfloat16)
    return jnp.where(numbers == row.astype(jnp.bfloat16), one, zero)


def place_kernel(bricks, groups, capacity, dest_ref, rows_ref, slot_ref, map_ref):
    width = dest_ref.shape[2]
    segments = dest_ref.shape[0] // groups
    room = map_ref.shape[2]
    upper = (
        lax.broadcasted_iota(jnp.int32, (width, width), 0)
        <= lax.broadcasted_iota(jnp.int32, (width, width), 1)
    )
    upper = jnp.where(upper, 1.0, 0.0).astype(jnp.bfloat16)
    ones = jnp.ones((width, width), jnp.bfloat16)

    def group(g, ignored):
        dests = [dest_ref[g * segments + s] for s in range(segments)]
        members = [one_hot_rows(bricks, dest) for dest in dests]
        stacked = jnp.concatenate(members, axis=0)
        within = dot(stacked, upper)
        totals = dot(stacked, ones)
        taken = jnp.zeros((bricks, width), jnp.float32)
        marked, ranks = [], []
        for s in range(segments):
            part = slice(s * bricks, (s + 1) * bricks)
            member = members[s].astype(jnp.float32)
            rank = jnp.sum(member * (within[part] + taken), axis=0, keepdims=True) - 1.0
            rank = rank.astype(jnp.int32)
            taken += totals[part]
            slot_ref[g * segments + s] = (dests[s] * groups + g) * capacity + rank
            row = (rows_ref[g * segments + s] + 1).astype(jnp.float32)
            marked.append((member * row).astype(jnp.bfloat16))
            ranks.append(one_hot_rows(room, rank))
        row_map = dot(jnp.concatenate(marked, axis=1), jnp.concatenate(ranks, axis=1), NT)
        map_ref[g] = row_map.astype(jnp.int32) - 1
        return ignored

    lax.fori_loop(0, groups, group, 0)


def score_kernel(chips, candidates, first, *refs):
    n = len(candidates)
    images, refs = refs[:n], refs[n:]
    proj_ref, refs = refs[0], refs[1:]
    if not first:
        norm_in, refs = refs[0], refs[4:]
    if first:
        norm_ref, refs = refs[0], refs[1:]
    else:
        norm_ref = norm_in
    p_hbm, x_hbm, stat_hbm, held, p_buf, stat_buf, sem_in, sem_p, sem_x, sem_s = refs
    block = held.shape[1]
    orients = proj_ref.shape[0]
    chunk = min(512, orients)
    me = lax.axis_index("ori")
    chip, core = me // 2, lax.rem(me, 2)
    plan = []
    for distance, direct, own in candidates:
        below = (core == 0) if direct else (core == 1)
        source = chip + jnp.where(below, -distance, distance)
        valid = jnp.logical_and(source >= 0, source < chips)
        plan.append((valid, jnp.clip(source, 0, chips - 1) * 2 + (core if own else 1 - core)))

    def copies(i):
        slot = plan[i][1]
        rows = pl.ds(pl.multiple_of(slot * block, block), block)
        return (
            lambda: pltpu.make_async_copy(images[i], held.at[i], sem_in.at[i]),
            lambda: pltpu.make_async_copy(held.at[i], x_hbm.at[rows], sem_x.at[i]),
            lambda: pltpu.make_async_copy(p_buf.at[i], p_hbm.at[slot], sem_p.at[i]),
            lambda: pltpu.make_async_copy(stat_buf.at[i], stat_hbm.at[slot], sem_s.at[i]),
        )

    for i in range(n):

        @pl.when(plan[i][0])
        def _(i=i):
            copies(i)[0]().start()

    if first:

        def square(r, ignored):
            rows = pl.ds(pl.multiple_of(r * chunk, chunk), chunk)
            values = proj_ref[rows, :].astype(jnp.float32)
            total = jnp.sum(values * values, axis=1, keepdims=True)
            norm_ref[rows, :] = jnp.broadcast_to(total, (chunk, norm_ref.shape[1]))
            return ignored

        lax.fori_loop(0, orients // chunk, square, 0)

    for i in range(n):

        @pl.when(plan[i][0])
        def _(i=i):
            fetch, keep, out, stats = copies(i)
            fetch().wait()
            keep().start()

            def score(r, largest):
                rows = pl.ds(pl.multiple_of(r * chunk, chunk), chunk)
                found = dot(proj_ref[rows, :], held[i], NT)
                norm = norm_ref[rows, 0:1]
                found = temper_scale * (found - 0.5 * norm)
                p_buf[i, rows, :] = found
                return jnp.maximum(largest, jnp.max(found, axis=0, keepdims=True))

            largest = lax.fori_loop(
                0, orients // chunk, score, jnp.full((1, block), -jnp.inf, jnp.float32)
            )

            def exponential(r, total):
                rows = pl.ds(pl.multiple_of(r * chunk, chunk), chunk)
                value = jnp.exp(p_buf[i, rows, :] - largest)
                p_buf[i, rows, :] = value
                return total + jnp.sum(value, axis=0, keepdims=True)

            total = lax.fori_loop(
                0, orients // chunk, exponential, jnp.zeros((1, block), jnp.float32)
            )
            out().start()
            pick = lax.broadcasted_iota(jnp.int32, (8, block), 0) == 0
            stat_buf[i] = jnp.where(pick, largest, total)
            stats().start()

    for i in range(n):

        @pl.when(plan[i][0])
        def _(i=i):
            for copy in copies(i)[1:]:
                copy().wait()


def score_step(chips, candidates, images, projections, carry):
    block, width = images[0].shape
    orients = projections.shape[0]
    blocks = 2 * chips
    n = len(candidates)
    first = carry is None
    shapes = [
        jax.ShapeDtypeStruct((blocks, orients, block), jnp.float32),
        jax.ShapeDtypeStruct((blocks * block, width), jnp.bfloat16),
        jax.ShapeDtypeStruct((blocks, 8, block), jnp.float32),
    ]
    in_specs = [ANY] * n + [VMEM]
    args = list(images) + [projections]
    if first:
        out_shape = [jax.ShapeDtypeStruct((orients, 128), jnp.float32)] + shapes
        out_specs = [VMEM] + [ANY] * 3
        aliases = {}
    else:
        in_specs += [VMEM] + [ANY] * 3
        args += list(carry)
        out_shape, out_specs = shapes, [ANY] * 3
        aliases = {n + 2 + k: k for k in range(3)}
    out = pl.pallas_call(
        functools.partial(score_kernel, chips, candidates, first),
        out_shape=out_shape,
        in_specs=in_specs,
        out_specs=out_specs,
        scratch_shapes=[
            pltpu.VMEM((n, block, width), jnp.bfloat16),
            pltpu.VMEM((n, orients, block), jnp.float32),
            pltpu.VMEM((n, 8, block), jnp.float32),
            pltpu.SemaphoreType.DMA((n,)),
            pltpu.SemaphoreType.DMA((n,)),
            pltpu.SemaphoreType.DMA((n,)),
            pltpu.SemaphoreType.DMA((n,)),
        ],
        input_output_aliases=aliases,
        compiler_params=pltpu.CompilerParams(vmem_limit_bytes=14 << 20),
        cost_estimate=pl.CostEstimate(flops=1000, bytes_accessed=1000, transcendentals=0),
        name="score_blocks",
    )(*args)
    return tuple(out) if first else (carry[0],) + tuple(out)


def merge_kernel(*refs):
    out_ref = refs[-1]
    for k in range(out_ref.shape[0]):
        sets = [ref[k] for ref in refs[:-1]]
        largest = functools.reduce(jnp.maximum, [a[0:1] for a in sets])
        total = sum(a[1:2] * jnp.exp(a[0:1] - largest) for a in sets)
        pick = lax.broadcasted_iota(jnp.int32, sets[0].shape, 0) == 0
        out_ref[k] = jnp.where(pick, largest, total)


def merge_step(*sets):
    return pl.pallas_call(
        merge_kernel,
        out_shape=jax.ShapeDtypeStruct(sets[0].shape, sets[0].dtype),
        in_specs=[VMEM] * len(sets),
        out_specs=VMEM,
        compiler_params=pltpu.CompilerParams(vmem_limit_bytes=4 << 20),
        cost_estimate=pl.CostEstimate(flops=1000, bytes_accessed=1000, transcendentals=0),
        name="merge_totals",
    )(*sets)


def sum_kernel(
    bricks,
    capacity,
    slot_ref,
    p_ref,
    stats_ref,
    totals_ref,
    x_ref,
    dest_ref,
    rows_ref,
    map_ref,
    other_ref,
    mine_ref,
    volume,
    weights,
    even,
    odd,
    slots,
):
    blocks, orients, block = p_ref.shape
    owned = dest_ref.shape[2]
    groups = orients // owned
    segments = dest_ref.shape[0] // groups
    per_tile = TILE // 128
    tiles = segments // per_tile
    core = lax.rem(lax.axis_index("ori"), 2)
    zero = jnp.zeros((512, 128), jnp.float32)

    def clear(i, ignored):
        slots[pl.ds(pl.multiple_of(i * 512, 512), 512), :] = zero
        return ignored

    lax.fori_loop(0, slots.shape[0] // 512, clear, 0)
    volume[...] = jnp.zeros_like(volume)

    def scatter(held, base):
        for s in range(per_tile):
            for r in range(owned // 8):
                values = held[r * 8 : r * 8 + 8, s * 128 : (s + 1) * 128]
                for k in range(8):
                    slot = slot_ref[base + s * owned + r * 8 + k]
                    slots[pl.ds(slot, 1), :] = values[k : k + 1, :]

    def product(t):
        columns = pl.ds(pl.multiple_of(t * TILE, TILE), TILE)
        return dot(weights[...], x_ref[:, columns])

    def group(g, ignored):
        rows = pl.ds(pl.multiple_of(g * owned, owned), owned)
        for k in range(blocks):
            scale = jnp.exp(stats_ref[k, 0:1] - totals_ref[k, 0:1]) / totals_ref[k, 1:2]
            weights[:, k * block : (k + 1) * block] = (p_ref[k, rows, :] * scale).astype(
                jnp.bfloat16
            )
        ones = jnp.ones((8, blocks * block), jnp.bfloat16)
        sums = dot(ones, weights[...], NT)[0:1]
        high = sums.astype(jnp.bfloat16).astype(jnp.float32)
        low = sums - high

        def weigh(s):
            dest = dest_ref[g * segments + s]
            member = lax.broadcasted_iota(jnp.int32, (bricks, owned), 0) == dest
            parts = [jnp.where(member, part, 0.0).astype(jnp.bfloat16) for part in (high, low)]
            landed = one_hot_rows(BRICK_ROWS, rows_ref[g * segments + s])
            return jnp.concatenate(parts, axis=0), landed

        def pair(j, ignored):
            both = [weigh(2 * j * per_tile + k) for k in range(2 * per_tile)]
            carried = jnp.concatenate([first for first, _ in both], axis=1)
            landed = jnp.concatenate([second for _, second in both], axis=1)
            volume[...] += dot(carried, landed, NT)
            base = (g * segments + 2 * j * per_tile) * owned
            even[...] = product(2 * j)
            scatter(odd, base)
            odd[...] = product(2 * j + 1)
            scatter(even, base + per_tile * owned)
            return ignored

        return lax.fori_loop(0, tiles // 2, pair, ignored)

    lax.fori_loop(0, groups, group, 0)
    scatter(odd, groups * segments * owned)
    span = map_ref.shape[2]

    def slots_of(i, parity):
        start = pl.multiple_of(brick_of(i, parity) * span, 8)
        return slots[pl.ds(start, span), :].astype(jnp.bfloat16)

    def keep(i, ignored):
        mine_ref[i] = slots_of(i, core)
        return ignored

    lax.fori_loop(0, bricks // 2, keep, 0)
    grid_bricks(1 - core, lambda i: slots_of(i, 1 - core), volume, map_ref, other_ref)


def brick_of(i, parity):
    chips = lax.axis_size("ori") // 2
    group = lax.bitwise_xor(lax.axis_index("img"), i // chips)
    chip = lax.bitwise_xor(lax.axis_index("ori") // 2, lax.rem(i, chips))
    return (group * chips + chip) * 2 + parity


def grid_bricks(parity, slots_of, volume, map_ref, out_ref):
    bricks = map_ref.shape[0]
    unroll = 8
    sub = lax.broadcasted_iota(jnp.int32, (EXTRA_ROWS, 128), 0)

    def grid_brick(i):
        b = brick_of(i, parity)
        cells = dot(one_hot_rows(BRICK_ROWS, map_ref[b]), slots_of(i))
        out_ref[i, 0:BRICK_ROWS, :] = cells.astype(out_ref.dtype)
        total = volume[pl.ds(b, 1), :] + volume[pl.ds(bricks + b, 1), :]
        top = total.astype(jnp.bfloat16).astype(jnp.float32)
        rest = total - top
        extra = jnp.where(sub == 0, top[:, :128], jnp.where(sub == 1, top[:, 128:], 0.0))
        extra += jnp.where(sub == 2, rest[:, :128], jnp.where(sub == 3, rest[:, 128:], 0.0))
        out_ref[i, BRICK_ROWS : BRICK_ROWS + EXTRA_ROWS, :] = extra.astype(out_ref.dtype)

    def step(i, ignored):
        for k in range(unroll):
            grid_brick(i * unroll + k)
        return ignored

    lax.fori_loop(0, bricks // 2 // unroll, step, 0)


def grid_kernel(slots, volume, map_ref, out_ref):
    core = lax.rem(lax.axis_index("ori"), 2)
    grid_bricks(core, lambda i: slots[i], volume, map_ref, out_ref)


def grid_step(slots, volume, row_map):
    bricks = row_map.shape[0]
    shape = (bricks // 2, BRICK_ROWS + EXTRA_ROWS, 128)
    return pl.pallas_call(
        grid_kernel,
        out_shape=jax.ShapeDtypeStruct(shape, jnp.float32),
        in_specs=[VMEM] * 3,
        out_specs=VMEM,
        compiler_params=pltpu.CompilerParams(vmem_limit_bytes=8 << 20),
        cost_estimate=pl.CostEstimate(flops=1000, bytes_accessed=1000, transcendentals=0),
        name="grid_own_bricks",
    )(slots, volume, row_map)


def sum_step(bricks, groups, capacity, slot, p, stats, totals, x, dest, rows, row_map):
    blocks, orients, block = p.shape
    width = x.shape[1]
    owned = orients // groups
    shape = (bricks // 2, BRICK_ROWS + EXTRA_ROWS, 128)
    return pl.pallas_call(
        functools.partial(sum_kernel, bricks, capacity),
        out_shape=[
            jax.ShapeDtypeStruct(shape, jnp.bfloat16),
            jax.ShapeDtypeStruct((bricks // 2, groups * capacity, 128), jnp.bfloat16),
            jax.ShapeDtypeStruct((2 * bricks, BRICK_ROWS), jnp.float32),
        ],
        in_specs=[SMEM] + [VMEM] * 7,
        out_specs=[VMEM] * 3,
        scratch_shapes=[
            pltpu.VMEM((owned, blocks * block), jnp.bfloat16),
            pltpu.VMEM((owned, TILE), jnp.float32),
            pltpu.VMEM((owned, TILE), jnp.float32),
            pltpu.VMEM((bricks * groups * capacity + 512, 128), jnp.float32),
        ],
        compiler_params=pltpu.CompilerParams(vmem_limit_bytes=19 << 20),
        cost_estimate=pl.CostEstimate(
            flops=2 * blocks * block * orients * width, bytes_accessed=24 << 20, transcendentals=0
        ),
        name="sum_and_grid",
    )(slot, p, stats, totals, x, dest, rows, row_map)


def body(images, projections, brick_dest, brick_rows, kernel):
    image_groups = lax.axis_size("img")
    orient_groups = lax.axis_size("ori")
    chips = orient_groups // 2
    bricks = image_groups * orient_groups
    orients, segments = brick_rows.shape
    owned = orients // image_groups
    capacity = max(2, 2 * owned * segments // bricks)
    me = lax.axis_index("ori")

    swap = [(i, i ^ 1) for i in range(orient_groups)]
    along = [(i, i + 2) for i in range(0, orient_groups - 2, 2)]
    along += [(i + 2, i) for i in range(1, orient_groups - 2, 2)]

    with jax.named_scope("place_segments"):

        def lanes(values):
            values = values.reshape(image_groups, owned, segments).transpose(0, 2, 1)
            return values.reshape(image_groups * segments, 1, owned)

        dest, rows = lanes(brick_dest), lanes(brick_rows)
        room = max(128, capacity)
        slot, row_map = pl.pallas_call(
            functools.partial(place_kernel, bricks, image_groups, capacity),
            out_shape=[
                jax.ShapeDtypeStruct(dest.shape, jnp.int32),
                jax.ShapeDtypeStruct((image_groups, bricks, room), jnp.int32),
            ],
            in_specs=[VMEM, VMEM],
            out_specs=[VMEM, VMEM],
            compiler_params=pltpu.CompilerParams(vmem_limit_bytes=8 << 20),
            cost_estimate=pl.CostEstimate(flops=1000, bytes_accessed=1000, transcendentals=0),
            name="place_segments",
        )(dest, rows)
        row_map = row_map[:, :, :capacity].transpose(1, 0, 2).reshape(bricks, 1, image_groups * capacity)
        unused = jnp.full(((TILE // 128) * owned,), bricks * image_groups * capacity, jnp.int32)
        placed = (jnp.concatenate([unused, slot.reshape(-1)]), row_map, dest, rows)

    with jax.named_scope("score"):
        mate = lax.ppermute(images, "ori", swap)
        moving = [images, mate]
        mate, placed = lax.optimization_barrier((mate, placed))
        carry = score_step(
            chips, ((0, True, True), (0, True, False)), (images, mate), projections, None
        )

        def arrive(distance, q, part):
            own = q == 0
            both = (part, lax.ppermute(part, "ori", swap))
            return ((distance, True, own), (distance, False, not own)), both

        def score(waiting, carry):
            return score_step(chips, waiting[0], waiting[1], projections, carry)

        waiting = []
        for distance in range(1, chips):
            moving = [lax.ppermute(part, "ori", along) for part in moving]
            for q in range(2):
                if distance == 1:
                    moving[q], carry = lax.optimization_barrier((moving[q], carry))
                elif distance == 2 and q == 0:
                    moving[q], carry = lax.optimization_barrier((moving[q], carry))
                else:
                    carry = score(waiting.pop(0), carry)
                    if distance == chips - 1 and q == 1:
                        carry = score(waiting.pop(0), carry)
                    moving[q], carry = lax.optimization_barrier((moving[q], carry))
                waiting.append(arrive(distance, q, moving[q]))
        late = [sum(parts, ()) for parts in zip(*waiting)]
        carry = score(late, carry)
        _, p, x, stats = carry
        slot, row_map, dest, rows = placed

    with jax.named_scope("softmax_total"):
        totals = merge_step(stats, lax.ppermute(stats, "ori", swap))
        others = [
            lax.ppermute(totals, "ori", [(i, i ^ (2 * k)) for i in range(orient_groups)])
            for k in range(1, chips)
        ]
        totals = merge_step(totals, *others)

    with jax.named_scope("sum_and_grid"):
        other_cells, slots, volume = sum_step(
            bricks, image_groups, capacity, slot, p, stats, totals, x, dest, rows, row_map
        )

    with jax.named_scope("brick_sums"):
        height = BRICK_ROWS + EXTRA_ROWS

        def add_up(cells, axis, ways, stride):
            total = cells[0].astype(jnp.float32)
            for k in range(1, ways):
                perm = [(i, i ^ (k * stride)) for i in range(ways * stride)]
                part = cells[k].astype(jnp.bfloat16)
                total += lax.ppermute(part, axis, perm).astype(jnp.float32)
            return total

        other_cells = lax.ppermute(other_cells, "ori", swap)
        cells = grid_step(slots, volume, row_map)
        cells = cells + other_cells.astype(jnp.float32)
        cells = cells.reshape(image_groups, chips, height, 128)
        cells = add_up(cells, "img", image_groups, 1)
        cells = add_up(cells, "ori", chips, 2)

    gridded = cells[:BRICK_ROWS]
    data_volume = jnp.dot(gridded, kernel[0].astype(jnp.float32), precision=lax.Precision.HIGHEST)
    extra = cells[BRICK_ROWS:]
    weight_volume = (extra[0:2] + extra[2:4]).reshape(1, BRICK_ROWS)
    return (data_volume[None], weight_volume)


def solution(mesh):
    placed = (
        P(("img", "ori"), None),
        P("ori", None),
        P("ori", None, None),
        P("ori", None),
        P(("img", "ori"), None, None),
    )
    return jax.shard_map(
        body,
        mesh=mesh,
        in_specs=placed,
        out_specs=(P(("img", "ori"), None, None), P(("img", "ori"), None)),
        check_vma=False,
    )
```

```python
import functools

import jax
import jax.numpy as jnp
from jax import lax
from jax.experimental import pallas as pl
from jax.experimental.pallas import tpu as pltpu
from jax.sharding import PartitionSpec as P

BRICK_ROWS = 256
EXTRA_ROWS = 16
TILE = 256
JOINED = 2
temper_scale = 4.0

ANY = pl.BlockSpec(memory_space=pl.ANY)
VMEM = pl.BlockSpec(memory_space=pltpu.VMEM)
SMEM = pl.BlockSpec(memory_space=pltpu.SMEM)
NN = (((1,), (0,)), ((), ()))
NT = (((1,), (1,)), ((), ()))


def dot(a, b, dims=NN):
    return lax.dot_general(a, b, dims, preferred_element_type=jnp.float32)


def one_hot_rows(count, row):
    numbers = lax.broadcasted_iota(jnp.int32, (count, row.shape[1]), 0).astype(jnp.bfloat16)
    one, zero = jnp.ones((), jnp.bfloat16), jnp.zeros((), jnp.bfloat16)
    return jnp.where(numbers == row.astype(jnp.bfloat16), one, zero)


def place_kernel(bricks, groups, capacity, dest_ref, rows_ref, slot_ref, map_ref):
    width = dest_ref.shape[2]
    segments = dest_ref.shape[0] // groups
    room = map_ref.shape[2]
    upper = (
        lax.broadcasted_iota(jnp.int32, (width, width), 0)
        <= lax.broadcasted_iota(jnp.int32, (width, width), 1)
    )
    upper = jnp.where(upper, 1.0, 0.0).astype(jnp.bfloat16)
    ones = jnp.ones((width, width), jnp.bfloat16)

    def group(g, ignored):
        dests = [dest_ref[g * segments + s] for s in range(segments)]
        members = [one_hot_rows(bricks, dest) for dest in dests]
        stacked = jnp.concatenate(members, axis=0)
        within = dot(stacked, upper)
        totals = dot(stacked, ones)
        taken = jnp.zeros((bricks, width), jnp.float32)
        marked, ranks = [], []
        for s in range(segments):
            part = slice(s * bricks, (s + 1) * bricks)
            member = members[s].astype(jnp.float32)
            rank = jnp.sum(member * (within[part] + taken), axis=0, keepdims=True) - 1.0
            rank = rank.astype(jnp.int32)
            taken += totals[part]
            slot_ref[g * segments + s] = (dests[s] * groups + g) * capacity + rank
            row = (rows_ref[g * segments + s] + 1).astype(jnp.float32)
            marked.append((member * row).astype(jnp.bfloat16))
            ranks.append(one_hot_rows(room, rank))
        row_map = dot(jnp.concatenate(marked, axis=1), jnp.concatenate(ranks, axis=1), NT)
        map_ref[g] = row_map.astype(jnp.int32) - 1
        return ignored

    lax.fori_loop(0, groups, group, 0)


def score_kernel(chips, candidates, first, *refs):
    n = len(candidates)
    images, refs = refs[:n], refs[n:]
    proj_ref, refs = refs[0], refs[1:]
    if first:
        norm_ref, p_ref, x_ref, stat_ref, sem = refs
    else:
        norm_ref, _, _, _, p_ref, x_ref, stat_ref, sem = refs
    block = images[0].shape[0]
    orients = proj_ref.shape[0]
    chunk = min(512, orients)
    me = lax.axis_index("ori")
    chip, core = me // 2, lax.rem(me, 2)
    plan = []
    for distance, direct, own in candidates:
        below = (core == 0) if direct else (core == 1)
        source = chip + jnp.where(below, -distance, distance)
        valid = jnp.logical_and(source >= 0, source < chips)
        plan.append((valid, jnp.clip(source, 0, chips - 1) * 2 + (core if own else 1 - core)))

    def keep(i):
        rows = pl.ds(pl.multiple_of(plan[i][1] * block, block), block)
        return pltpu.make_async_copy(images[i], x_ref.at[rows], sem.at[i])

    for i in range(n):

        @pl.when(plan[i][0])
        def _(i=i):
            keep(i).start()

    if first:

        def square(r, ignored):
            rows = pl.ds(pl.multiple_of(r * chunk, chunk), chunk)
            values = proj_ref[rows, :].astype(jnp.float32)
            total = jnp.sum(values * values, axis=1, keepdims=True)
            norm_ref[rows, :] = jnp.broadcast_to(total, (chunk, norm_ref.shape[1]))
            return ignored

        lax.fori_loop(0, orients // chunk, square, 0)

    for i in range(n):

        @pl.when(plan[i][0])
        def _(i=i):
            slot = plan[i][1]
            chunks = [slice(r, r + chunk) for r in range(0, orients, chunk)]
            largest = jnp.full((1, block), -jnp.inf, jnp.float32)
            for rows in chunks:
                found = dot(proj_ref[rows, :], images[i][...], NT)
                found = temper_scale * (found - 0.5 * norm_ref[rows, 0:1])
                p_ref[slot, rows, :] = found
                largest = jnp.maximum(largest, jnp.max(found, axis=0, keepdims=True))
            total = jnp.zeros((1, block), jnp.float32)
            for rows in chunks:
                value = jnp.exp(p_ref[slot, rows, :] - largest)
                p_ref[slot, rows, :] = value
                total += jnp.sum(value, axis=0, keepdims=True)
            pick = lax.broadcasted_iota(jnp.int32, (8, block), 0) == 0
            stat_ref[slot] = jnp.where(pick, largest, total)

    for i in range(n):

        @pl.when(plan[i][0])
        def _(i=i):
            keep(i).wait()


def score_step(chips, candidates, images, projections, carry):
    block, width = images[0].shape
    orients = projections.shape[0]
    blocks = 2 * chips
    n = len(candidates)
    first = carry is None
    shapes = [
        jax.ShapeDtypeStruct((blocks, orients, block), jnp.float32),
        jax.ShapeDtypeStruct((blocks * block, width), jnp.bfloat16),
        jax.ShapeDtypeStruct((blocks, 8, block), jnp.float32),
    ]
    in_specs = [VMEM] * (n + 1)
    args = list(images) + [projections]
    if first:
        out_shape = [jax.ShapeDtypeStruct((orients, 128), jnp.float32)] + shapes
        aliases = {}
    else:
        in_specs += [VMEM] * 4
        args += list(carry)
        out_shape = shapes
        aliases = {n + 2 + k: k for k in range(3)}
    out = pl.pallas_call(
        functools.partial(score_kernel, chips, candidates, first),
        out_shape=out_shape,
        in_specs=in_specs,
        out_specs=[VMEM] * len(out_shape),
        scratch_shapes=[pltpu.SemaphoreType.DMA((n,))],
        input_output_aliases=aliases,
        compiler_params=pltpu.CompilerParams(vmem_limit_bytes=10 << 20),
        cost_estimate=pl.CostEstimate(flops=1000, bytes_accessed=1000, transcendentals=0),
        name="score_blocks",
    )(*args)
    return tuple(out) if first else (carry[0],) + tuple(out)


def merge_kernel(*refs):
    out_ref = refs[-1]
    for k in range(out_ref.shape[0]):
        sets = [ref[k] for ref in refs[:-1]]
        largest = functools.reduce(jnp.maximum, [a[0:1] for a in sets])
        total = sum(a[1:2] * jnp.exp(a[0:1] - largest) for a in sets)
        pick = lax.broadcasted_iota(jnp.int32, sets[0].shape, 0) == 0
        out_ref[k] = jnp.where(pick, largest, total)


def merge_step(*sets):
    return pl.pallas_call(
        merge_kernel,
        out_shape=jax.ShapeDtypeStruct(sets[0].shape, sets[0].dtype),
        in_specs=[VMEM] * len(sets),
        out_specs=VMEM,
        compiler_params=pltpu.CompilerParams(vmem_limit_bytes=4 << 20),
        cost_estimate=pl.CostEstimate(flops=1000, bytes_accessed=1000, transcendentals=0),
        name="merge_totals",
    )(*sets)


def sum_kernel(
    bricks,
    capacity,
    slot_ref,
    p_ref,
    stats_ref,
    totals_ref,
    x_ref,
    dest_ref,
    rows_ref,
    map_ref,
    other_ref,
    mine_ref,
    volume,
    weights,
    even,
    odd,
    slots,
):
    blocks, orients, block = p_ref.shape
    owned = dest_ref.shape[2]
    taken = weights.shape[0]
    joined = taken // owned
    groups = orients // owned
    segments = dest_ref.shape[0] // groups
    per_tile = TILE // 128
    tiles = segments // per_tile
    core = lax.rem(lax.axis_index("ori"), 2)
    zero = jnp.zeros((512, 128), jnp.float32)

    def clear(i, ignored):
        slots[pl.ds(pl.multiple_of(i * 512, 512), 512), :] = zero
        return ignored

    lax.fori_loop(0, slots.shape[0] // 512, clear, 0)
    volume[...] = jnp.zeros_like(volume)

    def scatter(held, base):
        for s in range(per_tile):
            for r in range(taken // 8):
                values = held[r * 8 : r * 8 + 8, s * 128 : (s + 1) * 128]
                for k in range(8):
                    slot = slot_ref[base + s * taken + r * 8 + k]
                    slots[pl.ds(slot, 1), :] = values[k : k + 1, :]

    def product(t):
        columns = pl.ds(pl.multiple_of(t * TILE, TILE), TILE)
        return dot(weights[...], x_ref[:, columns])

    def group(g, ignored):
        rows = pl.ds(pl.multiple_of(g * taken, taken), taken)
        for k in range(blocks):
            scale = jnp.exp(stats_ref[k, 0:1] - totals_ref[k, 0:1]) / totals_ref[k, 1:2]
            weights[:, k * block : (k + 1) * block] = (p_ref[k, rows, :] * scale).astype(
                jnp.bfloat16
            )
        ones = jnp.ones((8, blocks * block), jnp.bfloat16)
        sums = dot(ones, weights[...], NT)[0:1]
        high = sums.astype(jnp.bfloat16).astype(jnp.float32)
        low = sums - high

        def weigh(s, h):
            lanes = slice(h * owned, (h + 1) * owned)
            at = (g * joined + h) * segments + s
            member = lax.broadcasted_iota(jnp.int32, (bricks, owned), 0) == dest_ref[at]
            parts = [
                jnp.where(member, part[:, lanes], 0.0).astype(jnp.bfloat16)
                for part in (high, low)
            ]
            landed = one_hot_rows(BRICK_ROWS, rows_ref[at])
            return jnp.concatenate(parts, axis=0), landed

        def pair(j, ignored):
            both = [
                weigh(2 * j * per_tile + k, h) for k in range(2 * per_tile) for h in range(joined)
            ]
            carried = jnp.concatenate([first for first, _ in both], axis=1)
            landed = jnp.concatenate([second for _, second in both], axis=1)
            volume[...] += dot(carried, landed, NT)
            base = (g * segments + 2 * j * per_tile) * taken
            even[...] = product(2 * j)
            scatter(odd, base)
            odd[...] = product(2 * j + 1)
            scatter(even, base + per_tile * taken)
            return ignored

        return lax.fori_loop(0, tiles // 2, pair, ignored)

    lax.fori_loop(0, groups // joined, group, 0)
    scatter(odd, groups * segments * owned)
    span = map_ref.shape[2]

    def slots_of(i, parity):
        start = pl.multiple_of(brick_of(i, parity) * span, 8)
        return slots[pl.ds(start, span), :].astype(jnp.bfloat16)

    def keep(i, ignored):
        mine_ref[i] = slots_of(i, core)
        return ignored

    lax.fori_loop(0, bricks // 2, keep, 0)
    grid_bricks(1 - core, lambda i: slots_of(i, 1 - core), volume, map_ref, other_ref)


def brick_of(i, parity):
    chips = lax.axis_size("ori") // 2
    group = lax.bitwise_xor(lax.axis_index("img"), i // chips)
    chip = lax.bitwise_xor(lax.axis_index("ori") // 2, lax.rem(i, chips))
    return (group * chips + chip) * 2 + parity


def grid_bricks(parity, slots_of, volume, map_ref, out_ref):
    bricks = map_ref.shape[0]
    unroll = 8
    sub = lax.broadcasted_iota(jnp.int32, (EXTRA_ROWS, 128), 0)

    def grid_brick(i):
        b = brick_of(i, parity)
        cells = dot(one_hot_rows(BRICK_ROWS, map_ref[b]), slots_of(i))
        out_ref[i, 0:BRICK_ROWS, :] = cells.astype(out_ref.dtype)
        total = volume[pl.ds(b, 1), :] + volume[pl.ds(bricks + b, 1), :]
        top = total.astype(jnp.bfloat16).astype(jnp.float32)
        rest = total - top
        extra = jnp.where(sub == 0, top[:, :128], jnp.where(sub == 1, top[:, 128:], 0.0))
        extra += jnp.where(sub == 2, rest[:, :128], jnp.where(sub == 3, rest[:, 128:], 0.0))
        out_ref[i, BRICK_ROWS : BRICK_ROWS + EXTRA_ROWS, :] = extra.astype(out_ref.dtype)

    def step(i, ignored):
        for k in range(unroll):
            grid_brick(i * unroll + k)
        return ignored

    lax.fori_loop(0, bricks // 2 // unroll, step, 0)


def grid_kernel(slots, volume, map_ref, out_ref):
    core = lax.rem(lax.axis_index("ori"), 2)
    grid_bricks(core, lambda i: slots[i], volume, map_ref, out_ref)


def grid_step(slots, volume, row_map):
    bricks = row_map.shape[0]
    shape = (bricks // 2, BRICK_ROWS + EXTRA_ROWS, 128)
    return pl.pallas_call(
        grid_kernel,
        out_shape=jax.ShapeDtypeStruct(shape, jnp.float32),
        in_specs=[VMEM] * 3,
        out_specs=VMEM,
        compiler_params=pltpu.CompilerParams(vmem_limit_bytes=8 << 20),
        cost_estimate=pl.CostEstimate(flops=1000, bytes_accessed=1000, transcendentals=0),
        name="grid_own_bricks",
    )(slots, volume, row_map)


def sum_step(bricks, groups, capacity, slot, p, stats, totals, x, dest, rows, row_map):
    blocks, orients, block = p.shape
    width = x.shape[1]
    owned = orients // groups
    joined = JOINED
    shape = (bricks // 2, BRICK_ROWS + EXTRA_ROWS, 128)
    return pl.pallas_call(
        functools.partial(sum_kernel, bricks, capacity),
        out_shape=[
            jax.ShapeDtypeStruct(shape, jnp.bfloat16),
            jax.ShapeDtypeStruct((bricks // 2, groups * capacity, 128), jnp.bfloat16),
            jax.ShapeDtypeStruct((2 * bricks, BRICK_ROWS), jnp.float32),
        ],
        in_specs=[SMEM] + [VMEM] * 7,
        out_specs=[VMEM] * 3,
        scratch_shapes=[
            pltpu.VMEM((joined * owned, blocks * block), jnp.bfloat16),
            pltpu.VMEM((joined * owned, TILE), jnp.float32),
            pltpu.VMEM((joined * owned, TILE), jnp.float32),
            pltpu.VMEM((bricks * groups * capacity + 512, 128), jnp.float32),
        ],
        compiler_params=pltpu.CompilerParams(vmem_limit_bytes=21 << 20),
        cost_estimate=pl.CostEstimate(
            flops=2 * blocks * block * orients * width, bytes_accessed=24 << 20, transcendentals=0
        ),
        name="sum_and_grid",
    )(slot, p, stats, totals, x, dest, rows, row_map)


def body(images, projections, brick_dest, brick_rows, kernel):
    image_groups = lax.axis_size("img")
    orient_groups = lax.axis_size("ori")
    chips = orient_groups // 2
    bricks = image_groups * orient_groups
    orients, segments = brick_rows.shape
    owned = orients // image_groups
    capacity = max(2, 2 * owned * segments // bricks)
    me = lax.axis_index("ori")

    swap = [(i, i ^ 1) for i in range(orient_groups)]
    along = [(i, i + 2) for i in range(0, orient_groups - 2, 2)]
    along += [(i + 2, i) for i in range(1, orient_groups - 2, 2)]

    with jax.named_scope("place_segments"):

        def lanes(values):
            values = values.reshape(image_groups, owned, segments).transpose(0, 2, 1)
            return values.reshape(image_groups * segments, 1, owned)

        dest, rows = lanes(brick_dest), lanes(brick_rows)
        room = max(128, capacity)
        slot, row_map = pl.pallas_call(
            functools.partial(place_kernel, bricks, image_groups, capacity),
            out_shape=[
                jax.ShapeDtypeStruct(dest.shape, jnp.int32),
                jax.ShapeDtypeStruct((image_groups, bricks, room), jnp.int32),
            ],
            in_specs=[VMEM, VMEM],
            out_specs=[VMEM, VMEM],
            compiler_params=pltpu.CompilerParams(vmem_limit_bytes=8 << 20),
            cost_estimate=pl.CostEstimate(flops=1000, bytes_accessed=1000, transcendentals=0),
            name="place_segments",
        )(dest, rows)
        row_map = row_map[:, :, :capacity].transpose(1, 0, 2).reshape(bricks, 1, image_groups * capacity)
        slot = slot.reshape(image_groups // JOINED, JOINED, segments, owned).transpose(0, 2, 1, 3)
        unused = jnp.full(
            ((TILE // 128) * JOINED * owned,), bricks * image_groups * capacity, jnp.int32
        )
        placed = (jnp.concatenate([unused, slot.reshape(-1)]), row_map, dest, rows)

    with jax.named_scope("score"):
        mate = lax.ppermute(images, "ori", swap)
        moving = [images, mate]
        mate, placed = lax.optimization_barrier((mate, placed))
        carry = score_step(
            chips, ((0, True, True), (0, True, False)), (images, mate), projections, None
        )

        def arrive(distance, q, part):
            own = q == 0
            both = (part, lax.ppermute(part, "ori", swap))
            return ((distance, True, own), (distance, False, not own)), both

        def score(waiting, carry):
            return score_step(chips, waiting[0], waiting[1], projections, carry)

        waiting = []
        for distance in range(1, chips):
            moving = [lax.ppermute(part, "ori", along) for part in moving]
            for q in range(2):
                if distance == 1:
                    moving[q], carry = lax.optimization_barrier((moving[q], carry))
                elif distance == 2 and q == 0:
                    moving[q], carry = lax.optimization_barrier((moving[q], carry))
                else:
                    carry = score(waiting.pop(0), carry)
                    if distance == chips - 1 and q == 1:
                        carry = score(waiting.pop(0), carry)
                    moving[q], carry = lax.optimization_barrier((moving[q], carry))
                waiting.append(arrive(distance, q, moving[q]))
        late = [sum(parts, ()) for parts in zip(*waiting)]
        carry = score(late, carry)
        _, p, x, stats = carry
        slot, row_map, dest, rows = placed

    with jax.named_scope("softmax_total"):
        totals = merge_step(stats, lax.ppermute(stats, "ori", swap))
        others = [
            lax.ppermute(totals, "ori", [(i, i ^ (2 * k)) for i in range(orient_groups)])
            for k in range(1, chips)
        ]
        totals = merge_step(totals, *others)

    with jax.named_scope("sum_and_grid"):
        other_cells, slots, volume = sum_step(
            bricks, image_groups, capacity, slot, p, stats, totals, x, dest, rows, row_map
        )

    with jax.named_scope("brick_sums"):
        height = BRICK_ROWS + EXTRA_ROWS

        def add_up(cells, axis, ways, stride):
            total = cells[0].astype(jnp.float32)
            for k in range(1, ways):
                perm = [(i, i ^ (k * stride)) for i in range(ways * stride)]
                part = cells[k].astype(jnp.bfloat16)
                total += lax.ppermute(part, axis, perm).astype(jnp.float32)
            return total

        other_cells = lax.ppermute(other_cells, "ori", swap)
        cells = grid_step(slots, volume, row_map)
        cells = cells + other_cells.astype(jnp.float32)
        cells = cells.reshape(image_groups, chips, height, 128)
        cells = add_up(cells, "img", image_groups, 1)
        cells = add_up(cells, "ori", chips, 2)

    gridded = cells[:BRICK_ROWS]
    data_volume = jnp.dot(gridded, kernel[0].astype(jnp.float32), precision=lax.Precision.HIGHEST)
    extra = cells[BRICK_ROWS:]
    weight_volume = (extra[0:2] + extra[2:4]).reshape(1, BRICK_ROWS)
    return (data_volume[None], weight_volume)


def solution(mesh):
    placed = (
        P(("img", "ori"), None),
        P("ori", None),
        P("ori", None, None),
        P("ori", None),
        P(("img", "ori"), None, None),
    )
    return jax.shard_map(
        body,
        mesh=mesh,
        in_specs=placed,
        out_specs=(P(("img", "ori"), None, None), P(("img", "ori"), None)),
        check_vma=False,
    )
```

```python
import functools

import jax
import jax.numpy as jnp
from jax import lax
from jax.experimental import pallas as pl
from jax.experimental.pallas import tpu as pltpu
from jax.sharding import PartitionSpec as P

BRICK_ROWS = 256
EXTRA_ROWS = 16
TILE = 256
JOINED = 2
temper_scale = 4.0

ANY = pl.BlockSpec(memory_space=pl.ANY)
VMEM = pl.BlockSpec(memory_space=pltpu.VMEM)
SMEM = pl.BlockSpec(memory_space=pltpu.SMEM)
NN = (((1,), (0,)), ((), ()))
NT = (((1,), (1,)), ((), ()))


def dot(a, b, dims=NN):
    return lax.dot_general(a, b, dims, preferred_element_type=jnp.float32)


def one_hot_rows(count, row):
    numbers = lax.broadcasted_iota(jnp.int32, (count, row.shape[1]), 0).astype(jnp.bfloat16)
    one, zero = jnp.ones((), jnp.bfloat16), jnp.zeros((), jnp.bfloat16)
    return jnp.where(numbers == row.astype(jnp.bfloat16), one, zero)


def place_kernel(bricks, groups, capacity, dest_ref, rows_ref, slot_ref, map_ref):
    width = dest_ref.shape[2]
    segments = dest_ref.shape[0] // groups
    room = map_ref.shape[2]
    upper = (
        lax.broadcasted_iota(jnp.int32, (width, width), 0)
        <= lax.broadcasted_iota(jnp.int32, (width, width), 1)
    )
    upper = jnp.where(upper, 1.0, 0.0).astype(jnp.bfloat16)
    ones = jnp.ones((width, width), jnp.bfloat16)

    def group(g, ignored):
        dests = [dest_ref[g * segments + s] for s in range(segments)]
        members = [one_hot_rows(bricks, dest) for dest in dests]
        stacked = jnp.concatenate(members, axis=0)
        within = dot(stacked, upper)
        totals = dot(stacked, ones)
        taken = jnp.zeros((bricks, width), jnp.float32)
        marked, ranks = [], []
        for s in range(segments):
            part = slice(s * bricks, (s + 1) * bricks)
            member = members[s].astype(jnp.float32)
            rank = jnp.sum(member * (within[part] + taken), axis=0, keepdims=True) - 1.0
            rank = rank.astype(jnp.int32)
            taken += totals[part]
            slot_ref[g * segments + s] = (dests[s] * groups + g) * capacity + rank
            row = (rows_ref[g * segments + s] + 1).astype(jnp.float32)
            marked.append((member * row).astype(jnp.bfloat16))
            ranks.append(one_hot_rows(room, rank))
        row_map = dot(jnp.concatenate(marked, axis=1), jnp.concatenate(ranks, axis=1), NT)
        map_ref[g] = row_map.astype(jnp.int32) - 1
        return ignored

    lax.fori_loop(0, groups, group, 0)


def score_kernel(chips, candidates, first, *refs):
    n = len(candidates)
    images, refs = refs[:n], refs[n:]
    proj_ref, refs = refs[0], refs[1:]
    if first:
        norm_ref, p_ref, x_ref, stat_ref, sem = refs
    else:
        norm_ref, _, _, _, p_ref, x_ref, stat_ref, sem = refs
    block = images[0].shape[0]
    orients = proj_ref.shape[0]
    chunk = min(512, orients)
    me = lax.axis_index("ori")
    chip, core = me // 2, lax.rem(me, 2)
    plan = []
    for distance, direct, own in candidates:
        below = (core == 0) if direct else (core == 1)
        source = chip + jnp.where(below, -distance, distance)
        valid = jnp.logical_and(source >= 0, source < chips)
        plan.append((valid, jnp.clip(source, 0, chips - 1) * 2 + (core if own else 1 - core)))

    def keep(i):
        rows = pl.ds(pl.multiple_of(plan[i][1] * block, block), block)
        return pltpu.make_async_copy(images[i], x_ref.at[rows], sem.at[i])

    for i in range(n):

        @pl.when(plan[i][0])
        def _(i=i):
            keep(i).start()

    if first:

        def square(r, ignored):
            rows = pl.ds(pl.multiple_of(r * chunk, chunk), chunk)
            values = proj_ref[rows, :].astype(jnp.float32)
            total = jnp.sum(values * values, axis=1, keepdims=True)
            norm_ref[rows, :] = jnp.broadcast_to(total, (chunk, norm_ref.shape[1]))
            return ignored

        lax.fori_loop(0, orients // chunk, square, 0)

    for i in range(n):

        @pl.when(plan[i][0])
        def _(i=i):
            slot = plan[i][1]
            chunks = [slice(r, r + chunk) for r in range(0, orients, chunk)]
            largest = jnp.full((1, block), -jnp.inf, jnp.float32)
            for rows in chunks:
                found = dot(proj_ref[rows, :], images[i][...], NT)
                found = temper_scale * (found - 0.5 * norm_ref[rows, 0:1])
                p_ref[slot, rows, :] = found
                largest = jnp.maximum(largest, jnp.max(found, axis=0, keepdims=True))
            total = jnp.zeros((1, block), jnp.float32)
            for rows in chunks:
                value = jnp.exp(p_ref[slot, rows, :] - largest)
                p_ref[slot, rows, :] = value
                total += jnp.sum(value, axis=0, keepdims=True)
            pick = lax.broadcasted_iota(jnp.int32, (2, block), 0) == 0
            stat_ref[slot] = jnp.where(pick, largest, total)

    for i in range(n):

        @pl.when(plan[i][0])
        def _(i=i):
            keep(i).wait()


def score_step(chips, candidates, images, projections, carry):
    block, width = images[0].shape
    orients = projections.shape[0]
    blocks = 2 * chips
    n = len(candidates)
    first = carry is None
    shapes = [
        jax.ShapeDtypeStruct((blocks, orients, block), jnp.float32),
        jax.ShapeDtypeStruct((blocks * block, width), jnp.bfloat16),
        jax.ShapeDtypeStruct((blocks, 2, block), jnp.float32),
    ]
    in_specs = [VMEM] * (n + 1)
    args = list(images) + [projections]
    if first:
        out_shape = [jax.ShapeDtypeStruct((orients, 128), jnp.float32)] + shapes
        aliases = {}
    else:
        in_specs += [VMEM] * 4
        args += list(carry)
        out_shape = shapes
        aliases = {n + 2 + k: k for k in range(3)}
    out = pl.pallas_call(
        functools.partial(score_kernel, chips, candidates, first),
        out_shape=out_shape,
        in_specs=in_specs,
        out_specs=[VMEM] * len(out_shape),
        scratch_shapes=[pltpu.SemaphoreType.DMA((n,))],
        input_output_aliases=aliases,
        compiler_params=pltpu.CompilerParams(vmem_limit_bytes=10 << 20),
        cost_estimate=pl.CostEstimate(flops=1000, bytes_accessed=1000, transcendentals=0),
        name="score_blocks",
    )(*args)
    return tuple(out) if first else (carry[0],) + tuple(out)


def merge_kernel(*refs):
    out_ref = refs[-1]
    for k in range(out_ref.shape[0]):
        sets = [ref[k] for ref in refs[:-1]]
        largest = functools.reduce(jnp.maximum, [a[0:1] for a in sets])
        total = sum(a[1:2] * jnp.exp(a[0:1] - largest) for a in sets)
        pick = lax.broadcasted_iota(jnp.int32, sets[0].shape, 0) == 0
        out_ref[k] = jnp.where(pick, largest, total)


def merge_step(*sets):
    return pl.pallas_call(
        merge_kernel,
        out_shape=jax.ShapeDtypeStruct(sets[0].shape, sets[0].dtype),
        in_specs=[VMEM] * len(sets),
        out_specs=VMEM,
        compiler_params=pltpu.CompilerParams(vmem_limit_bytes=4 << 20),
        cost_estimate=pl.CostEstimate(flops=1000, bytes_accessed=1000, transcendentals=0),
        name="merge_totals",
    )(*sets)


def sum_kernel(
    bricks,
    capacity,
    slot_ref,
    p_ref,
    stats_ref,
    totals_ref,
    x_ref,
    dest_ref,
    rows_ref,
    map_ref,
    other_ref,
    mine_ref,
    volume,
    weights,
    even,
    odd,
    slots,
):
    blocks, orients, block = p_ref.shape
    owned = dest_ref.shape[2]
    taken = weights.shape[0]
    joined = taken // owned
    groups = orients // owned
    segments = dest_ref.shape[0] // groups
    per_tile = TILE // 128
    tiles = segments // per_tile
    core = lax.rem(lax.axis_index("ori"), 2)
    zero = jnp.zeros((512, 128), jnp.float32)

    def clear(i, ignored):
        slots[pl.ds(pl.multiple_of(i * 512, 512), 512), :] = zero
        return ignored

    lax.fori_loop(0, slots.shape[0] // 512, clear, 0)
    volume[...] = jnp.zeros_like(volume)

    def scatter(held, base):
        for s in range(per_tile):
            for r in range(taken // 8):
                values = held[r * 8 : r * 8 + 8, s * 128 : (s + 1) * 128]
                for k in range(8):
                    slot = slot_ref[base + s * taken + r * 8 + k]
                    slots[pl.ds(slot, 1), :] = values[k : k + 1, :]

    def product(t):
        columns = pl.ds(pl.multiple_of(t * TILE, TILE), TILE)
        return dot(weights[...], x_ref[:, columns])

    def group(g, ignored):
        rows = pl.ds(pl.multiple_of(g * taken, taken), taken)
        for k in range(blocks):
            scale = jnp.exp(stats_ref[k, 0:1] - totals_ref[k, 0:1]) / totals_ref[k, 1:2]
            weights[:, k * block : (k + 1) * block] = (p_ref[k, rows, :] * scale).astype(
                jnp.bfloat16
            )
        ones = jnp.ones((8, blocks * block), jnp.bfloat16)
        sums = dot(ones, weights[...], NT)[0:1]
        high = sums.astype(jnp.bfloat16).astype(jnp.float32)
        low = sums - high

        def weigh(s, h):
            lanes = slice(h * owned, (h + 1) * owned)
            at = (g * joined + h) * segments + s
            member = lax.broadcasted_iota(jnp.int32, (bricks, owned), 0) == dest_ref[at]
            parts = [
                jnp.where(member, part[:, lanes], 0.0).astype(jnp.bfloat16)
                for part in (high, low)
            ]
            landed = one_hot_rows(BRICK_ROWS, rows_ref[at])
            return jnp.concatenate(parts, axis=0), landed

        def pair(j, ignored):
            both = [
                weigh(2 * j * per_tile + k, h) for k in range(2 * per_tile) for h in range(joined)
            ]
            carried = jnp.concatenate([first for first, _ in both], axis=1)
            landed = jnp.concatenate([second for _, second in both], axis=1)
            volume[...] += dot(carried, landed, NT)
            base = (g * segments + 2 * j * per_tile) * taken
            even[...] = product(2 * j)
            scatter(odd, base)
            odd[...] = product(2 * j + 1)
            scatter(even, base + per_tile * taken)
            return ignored

        return lax.fori_loop(0, tiles // 2, pair, ignored)

    lax.fori_loop(0, groups // joined, group, 0)
    scatter(odd, groups * segments * owned)
    span = map_ref.shape[2]

    def slots_of(i, parity):
        start = pl.multiple_of(brick_of(i, parity) * span, 8)
        return slots[pl.ds(start, span), :].astype(jnp.bfloat16)

    def keep(i, ignored):
        mine_ref[i] = slots_of(i, core)
        return ignored

    lax.fori_loop(0, bricks // 2, keep, 0)
    grid_bricks(1 - core, lambda i: slots_of(i, 1 - core), volume, map_ref, other_ref)


def brick_of(i, parity):
    chips = lax.axis_size("ori") // 2
    group = lax.bitwise_xor(lax.axis_index("img"), i // chips)
    chip = lax.bitwise_xor(lax.axis_index("ori") // 2, lax.rem(i, chips))
    return (group * chips + chip) * 2 + parity


def grid_bricks(parity, slots_of, volume, map_ref, out_ref):
    bricks = map_ref.shape[0]
    unroll = min(16, bricks // 2)
    sub = lax.broadcasted_iota(jnp.int32, (EXTRA_ROWS, 128), 0)

    def grid_brick(i):
        b = brick_of(i, parity)
        cells = dot(one_hot_rows(BRICK_ROWS, map_ref[b]), slots_of(i))
        out_ref[i, 0:BRICK_ROWS, :] = cells.astype(out_ref.dtype)
        total = volume[pl.ds(b, 1), :] + volume[pl.ds(bricks + b, 1), :]
        top = total.astype(jnp.bfloat16).astype(jnp.float32)
        rest = total - top
        extra = jnp.where(sub == 0, top[:, :128], jnp.where(sub == 1, top[:, 128:], 0.0))
        extra += jnp.where(sub == 2, rest[:, :128], jnp.where(sub == 3, rest[:, 128:], 0.0))
        out_ref[i, BRICK_ROWS : BRICK_ROWS + EXTRA_ROWS, :] = extra.astype(out_ref.dtype)

    def step(i, ignored):
        for k in range(unroll):
            grid_brick(i * unroll + k)
        return ignored

    lax.fori_loop(0, bricks // 2 // unroll, step, 0)


def grid_kernel(slots, volume, map_ref, out_ref):
    core = lax.rem(lax.axis_index("ori"), 2)
    grid_bricks(core, lambda i: slots[i], volume, map_ref, out_ref)


def grid_step(slots, volume, row_map):
    bricks = row_map.shape[0]
    shape = (bricks // 2, BRICK_ROWS + EXTRA_ROWS, 128)
    return pl.pallas_call(
        grid_kernel,
        out_shape=jax.ShapeDtypeStruct(shape, jnp.float32),
        in_specs=[VMEM] * 3,
        out_specs=VMEM,
        compiler_params=pltpu.CompilerParams(vmem_limit_bytes=8 << 20),
        cost_estimate=pl.CostEstimate(flops=1000, bytes_accessed=1000, transcendentals=0),
        name="grid_own_bricks",
    )(slots, volume, row_map)


def sum_step(bricks, groups, capacity, slot, p, stats, totals, x, dest, rows, row_map):
    blocks, orients, block = p.shape
    width = x.shape[1]
    owned = orients // groups
    joined = JOINED
    shape = (bricks // 2, BRICK_ROWS + EXTRA_ROWS, 128)
    return pl.pallas_call(
        functools.partial(sum_kernel, bricks, capacity),
        out_shape=[
            jax.ShapeDtypeStruct(shape, jnp.bfloat16),
            jax.ShapeDtypeStruct((bricks // 2, groups * capacity, 128), jnp.bfloat16),
            jax.ShapeDtypeStruct((2 * bricks, BRICK_ROWS), jnp.float32),
        ],
        in_specs=[SMEM] + [VMEM] * 7,
        out_specs=[VMEM] * 3,
        scratch_shapes=[
            pltpu.VMEM((joined * owned, blocks * block), jnp.bfloat16),
            pltpu.VMEM((joined * owned, TILE), jnp.float32),
            pltpu.VMEM((joined * owned, TILE), jnp.float32),
            pltpu.VMEM((bricks * groups * capacity + 512, 128), jnp.float32),
        ],
        compiler_params=pltpu.CompilerParams(vmem_limit_bytes=21 << 20),
        cost_estimate=pl.CostEstimate(
            flops=2 * blocks * block * orients * width, bytes_accessed=24 << 20, transcendentals=0
        ),
        name="sum_and_grid",
    )(slot, p, stats, totals, x, dest, rows, row_map)


def body(images, projections, brick_dest, brick_rows, kernel):
    image_groups = lax.axis_size("img")
    orient_groups = lax.axis_size("ori")
    chips = orient_groups // 2
    bricks = image_groups * orient_groups
    orients, segments = brick_rows.shape
    owned = orients // image_groups
    capacity = max(2, 2 * owned * segments // bricks)
    me = lax.axis_index("ori")

    swap = [(i, i ^ 1) for i in range(orient_groups)]
    along = [(i, i + 2) for i in range(0, orient_groups - 2, 2)]
    along += [(i + 2, i) for i in range(1, orient_groups - 2, 2)]

    with jax.named_scope("place_segments"):

        def lanes(values):
            values = values.reshape(image_groups, owned, segments).transpose(0, 2, 1)
            return values.reshape(image_groups * segments, 1, owned)

        dest, rows = lanes(brick_dest), lanes(brick_rows)
        room = max(128, capacity)
        slot, row_map = pl.pallas_call(
            functools.partial(place_kernel, bricks, image_groups, capacity),
            out_shape=[
                jax.ShapeDtypeStruct(dest.shape, jnp.int32),
                jax.ShapeDtypeStruct((image_groups, bricks, room), jnp.int32),
            ],
            in_specs=[VMEM, VMEM],
            out_specs=[VMEM, VMEM],
            compiler_params=pltpu.CompilerParams(vmem_limit_bytes=8 << 20),
            cost_estimate=pl.CostEstimate(flops=1000, bytes_accessed=1000, transcendentals=0),
            name="place_segments",
        )(dest, rows)
        row_map = row_map[:, :, :capacity].transpose(1, 0, 2).reshape(bricks, 1, image_groups * capacity)
        slot = slot.reshape(image_groups // JOINED, JOINED, segments, owned).transpose(0, 2, 1, 3)
        unused = jnp.full(
            ((TILE // 128) * JOINED * owned,), bricks * image_groups * capacity, jnp.int32
        )
        placed = (jnp.concatenate([unused, slot.reshape(-1)]), row_map, dest, rows)

    with jax.named_scope("score"):
        mate = lax.ppermute(images, "ori", swap)
        moving = [images, mate]
        mate, placed = lax.optimization_barrier((mate, placed))
        carry = score_step(
            chips, ((0, True, True), (0, True, False)), (images, mate), projections, None
        )

        def arrive(distance, q, part):
            own = q == 0
            both = (part, lax.ppermute(part, "ori", swap))
            return ((distance, True, own), (distance, False, not own)), both

        def score(waiting, carry):
            return score_step(chips, waiting[0], waiting[1], projections, carry)

        waiting = []
        for distance in range(1, chips):
            moving = [lax.ppermute(part, "ori", along) for part in moving]
            for q in range(2):
                if distance == 1:
                    moving[q], carry = lax.optimization_barrier((moving[q], carry))
                elif distance == 2 and q == 0:
                    moving[q], carry = lax.optimization_barrier((moving[q], carry))
                else:
                    carry = score(waiting.pop(0), carry)
                    if distance == chips - 1 and q == 1:
                        carry = score(waiting.pop(0), carry)
                    moving[q], carry = lax.optimization_barrier((moving[q], carry))
                waiting.append(arrive(distance, q, moving[q]))
        late = [sum(parts, ()) for parts in zip(*waiting)]
        carry = score(late, carry)
        _, p, x, stats = carry
        slot, row_map, dest, rows = placed

    with jax.named_scope("softmax_total"):
        totals = merge_step(stats, lax.ppermute(stats, "ori", swap))
        others = [
            lax.ppermute(totals, "ori", [(i, i ^ (2 * k)) for i in range(orient_groups)])
            for k in range(1, chips)
        ]
        totals = merge_step(totals, *others)

    with jax.named_scope("sum_and_grid"):
        other_cells, slots, volume = sum_step(
            bricks, image_groups, capacity, slot, p, stats, totals, x, dest, rows, row_map
        )

    with jax.named_scope("brick_sums"):
        height = BRICK_ROWS + EXTRA_ROWS

        def add_up(cells, axis, ways, stride):
            total = cells[0].astype(jnp.float32)
            for k in range(1, ways):
                perm = [(i, i ^ (k * stride)) for i in range(ways * stride)]
                part = cells[k].astype(jnp.bfloat16)
                total += lax.ppermute(part, axis, perm).astype(jnp.float32)
            return total

        other_cells = lax.ppermute(other_cells, "ori", swap)
        cells = grid_step(slots, volume, row_map)
        cells = cells + other_cells.astype(jnp.float32)
        cells = cells.reshape(image_groups, chips, height, 128)
        cells = add_up(cells, "img", image_groups, 1)
        cells = add_up(cells, "ori", chips, 2)

    gridded = cells[:BRICK_ROWS]
    data_volume = jnp.dot(gridded, kernel[0].astype(jnp.float32), precision=lax.Precision.HIGHEST)
    extra = cells[BRICK_ROWS:]
    weight_volume = (extra[0:2] + extra[2:4]).reshape(1, BRICK_ROWS)
    return (data_volume[None], weight_volume)


def solution(mesh):
    placed = (
        P(("img", "ori"), None),
        P("ori", None),
        P("ori", None, None),
        P("ori", None),
        P(("img", "ori"), None, None),
    )
    return jax.shard_map(
        body,
        mesh=mesh,
        in_specs=placed,
        out_specs=(P(("img", "ori"), None, None), P(("img", "ori"), None)),
        check_vma=False,
    )
```

```python
import functools

import jax
import jax.numpy as jnp
from jax import lax
from jax.experimental import pallas as pl
from jax.experimental.pallas import tpu as pltpu
from jax.sharding import PartitionSpec as P

BRICK_ROWS = 256
EXTRA_ROWS = 16
TILE = 512
JOINED = 2
temper_scale = 4.0

ANY = pl.BlockSpec(memory_space=pl.ANY)
VMEM = pl.BlockSpec(memory_space=pltpu.VMEM)
SMEM = pl.BlockSpec(memory_space=pltpu.SMEM)
NN = (((1,), (0,)), ((), ()))
NT = (((1,), (1,)), ((), ()))


def dot(a, b, dims=NN):
    return lax.dot_general(a, b, dims, preferred_element_type=jnp.float32)


def one_hot_rows(count, row):
    numbers = lax.broadcasted_iota(jnp.int32, (count, row.shape[1]), 0).astype(jnp.bfloat16)
    one, zero = jnp.ones((), jnp.bfloat16), jnp.zeros((), jnp.bfloat16)
    return jnp.where(numbers == row.astype(jnp.bfloat16), one, zero)


def place_kernel(bricks, groups, capacity, dest_ref, rows_ref, slot_ref, map_ref):
    width = dest_ref.shape[2]
    segments = dest_ref.shape[0] // groups
    room = map_ref.shape[2]
    upper = (
        lax.broadcasted_iota(jnp.int32, (width, width), 0)
        <= lax.broadcasted_iota(jnp.int32, (width, width), 1)
    )
    upper = jnp.where(upper, 1.0, 0.0).astype(jnp.bfloat16)
    ones = jnp.ones((width, width), jnp.bfloat16)

    def group(g, ignored):
        dests = [dest_ref[g * segments + s] for s in range(segments)]
        members = [one_hot_rows(bricks, dest) for dest in dests]
        stacked = jnp.concatenate(members, axis=0)
        within = dot(stacked, upper)
        totals = dot(stacked, ones)
        taken = jnp.zeros((bricks, width), jnp.float32)
        marked, ranks = [], []
        for s in range(segments):
            part = slice(s * bricks, (s + 1) * bricks)
            member = members[s].astype(jnp.float32)
            rank = jnp.sum(member * (within[part] + taken), axis=0, keepdims=True) - 1.0
            rank = rank.astype(jnp.int32)
            taken += totals[part]
            slot_ref[g * segments + s] = (dests[s] * groups + g) * capacity + rank
            row = (rows_ref[g * segments + s] + 1).astype(jnp.float32)
            marked.append((member * row).astype(jnp.bfloat16))
            ranks.append(one_hot_rows(room, rank))
        row_map = dot(jnp.concatenate(marked, axis=1), jnp.concatenate(ranks, axis=1), NT)
        map_ref[g] = row_map.astype(jnp.int32) - 1
        return ignored

    lax.fori_loop(0, groups, group, 0)


def score_kernel(chips, candidates, first, *refs):
    n = len(candidates)
    images, refs = refs[:n], refs[n:]
    proj_ref, refs = refs[0], refs[1:]
    if first:
        norm_ref, p_ref, x_ref, stat_ref, sem = refs
    else:
        norm_ref, _, _, _, p_ref, x_ref, stat_ref, sem = refs
    block = images[0].shape[0]
    orients = proj_ref.shape[0]
    chunk = min(512, orients)
    me = lax.axis_index("ori")
    chip, core = me // 2, lax.rem(me, 2)
    plan = []
    for distance, direct, own in candidates:
        below = (core == 0) if direct else (core == 1)
        source = chip + jnp.where(below, -distance, distance)
        valid = jnp.logical_and(source >= 0, source < chips)
        plan.append((valid, jnp.clip(source, 0, chips - 1) * 2 + (core if own else 1 - core)))

    def keep(i):
        rows = pl.ds(pl.multiple_of(plan[i][1] * block, block), block)
        return pltpu.make_async_copy(images[i], x_ref.at[rows], sem.at[i])

    for i in range(n):

        @pl.when(plan[i][0])
        def _(i=i):
            keep(i).start()

    if first:

        def square(r, ignored):
            rows = pl.ds(pl.multiple_of(r * chunk, chunk), chunk)
            values = proj_ref[rows, :].astype(jnp.float32)
            total = jnp.sum(values * values, axis=1, keepdims=True)
            norm_ref[rows, :] = jnp.broadcast_to(total, (chunk, norm_ref.shape[1]))
            return ignored

        lax.fori_loop(0, orients // chunk, square, 0)

    for i in range(n):

        @pl.when(plan[i][0])
        def _(i=i):
            slot = plan[i][1]
            chunks = [slice(r, r + chunk) for r in range(0, orients, chunk)]
            largest = jnp.full((1, block), -jnp.inf, jnp.float32)
            for rows in chunks:
                found = dot(proj_ref[rows, :], images[i][...], NT)
                found = temper_scale * (found - 0.5 * norm_ref[rows, 0:1])
                p_ref[slot, rows, :] = found
                largest = jnp.maximum(largest, jnp.max(found, axis=0, keepdims=True))
            total = jnp.zeros((1, block), jnp.float32)
            for rows in chunks:
                value = jnp.exp(p_ref[slot, rows, :] - largest)
                p_ref[slot, rows, :] = value
                total += jnp.sum(value, axis=0, keepdims=True)
            pick = lax.broadcasted_iota(jnp.int32, (2, block), 0) == 0
            stat_ref[slot] = jnp.where(pick, largest, total)

    for i in range(n):

        @pl.when(plan[i][0])
        def _(i=i):
            keep(i).wait()


def score_step(chips, candidates, images, projections, carry):
    block, width = images[0].shape
    orients = projections.shape[0]
    blocks = 2 * chips
    n = len(candidates)
    first = carry is None
    shapes = [
        jax.ShapeDtypeStruct((blocks, orients, block), jnp.float32),
        jax.ShapeDtypeStruct((blocks * block, width), jnp.bfloat16),
        jax.ShapeDtypeStruct((blocks, 2, block), jnp.float32),
    ]
    in_specs = [VMEM] * (n + 1)
    args = list(images) + [projections]
    if first:
        out_shape = [jax.ShapeDtypeStruct((orients, 128), jnp.float32)] + shapes
        aliases = {}
    else:
        in_specs += [VMEM] * 4
        args += list(carry)
        out_shape = shapes
        aliases = {n + 2 + k: k for k in range(3)}
    out = pl.pallas_call(
        functools.partial(score_kernel, chips, candidates, first),
        out_shape=out_shape,
        in_specs=in_specs,
        out_specs=[VMEM] * len(out_shape),
        scratch_shapes=[pltpu.SemaphoreType.DMA((n,))],
        input_output_aliases=aliases,
        compiler_params=pltpu.CompilerParams(vmem_limit_bytes=10 << 20),
        cost_estimate=pl.CostEstimate(flops=1000, bytes_accessed=1000, transcendentals=0),
        name="score_blocks",
    )(*args)
    return tuple(out) if first else (carry[0],) + tuple(out)


def merge_kernel(*refs):
    out_ref = refs[-1]
    for k in range(out_ref.shape[0]):
        sets = [ref[k] for ref in refs[:-1]]
        largest = functools.reduce(jnp.maximum, [a[0:1] for a in sets])
        total = sum(a[1:2] * jnp.exp(a[0:1] - largest) for a in sets)
        pick = lax.broadcasted_iota(jnp.int32, sets[0].shape, 0) == 0
        out_ref[k] = jnp.where(pick, largest, total)


def merge_step(*sets):
    return pl.pallas_call(
        merge_kernel,
        out_shape=jax.ShapeDtypeStruct(sets[0].shape, sets[0].dtype),
        in_specs=[VMEM] * len(sets),
        out_specs=VMEM,
        compiler_params=pltpu.CompilerParams(vmem_limit_bytes=4 << 20),
        cost_estimate=pl.CostEstimate(flops=1000, bytes_accessed=1000, transcendentals=0),
        name="merge_totals",
    )(*sets)


def sum_kernel(
    bricks,
    capacity,
    slot_ref,
    p_ref,
    stats_ref,
    totals_ref,
    x_ref,
    dest_ref,
    rows_ref,
    map_ref,
    other_ref,
    mine_ref,
    volume,
    weights,
    even,
    odd,
    slots,
):
    blocks, orients, block = p_ref.shape
    owned = dest_ref.shape[2]
    taken = weights.shape[0]
    joined = taken // owned
    groups = orients // owned
    segments = dest_ref.shape[0] // groups
    per_tile = TILE // 128
    tiles = segments // per_tile
    core = lax.rem(lax.axis_index("ori"), 2)
    zero = jnp.zeros((512, 128), jnp.float32)

    def clear(i, ignored):
        slots[pl.ds(pl.multiple_of(i * 512, 512), 512), :] = zero
        return ignored

    lax.fori_loop(0, slots.shape[0] // 512, clear, 0)
    volume[...] = jnp.zeros_like(volume)

    def scatter(held, base):
        for s in range(per_tile):
            for r in range(taken // 8):
                values = held[r * 8 : r * 8 + 8, s * 128 : (s + 1) * 128]
                for k in range(8):
                    slot = slot_ref[base + s * taken + r * 8 + k]
                    slots[pl.ds(slot, 1), :] = values[k : k + 1, :]

    def product(t):
        columns = pl.ds(pl.multiple_of(t * TILE, TILE), TILE)
        return dot(weights[...], x_ref[:, columns])

    def group(g, ignored):
        rows = pl.ds(pl.multiple_of(g * taken, taken), taken)
        for k in range(blocks):
            scale = jnp.exp(stats_ref[k, 0:1] - totals_ref[k, 0:1]) / totals_ref[k, 1:2]
            weights[:, k * block : (k + 1) * block] = (p_ref[k, rows, :] * scale).astype(
                jnp.bfloat16
            )
        ones = jnp.ones((8, blocks * block), jnp.bfloat16)
        sums = dot(ones, weights[...], NT)[0:1]
        high = sums.astype(jnp.bfloat16).astype(jnp.float32)
        low = sums - high

        def weigh(s, h):
            lanes = slice(h * owned, (h + 1) * owned)
            at = (g * joined + h) * segments + s
            member = lax.broadcasted_iota(jnp.int32, (bricks, owned), 0) == dest_ref[at]
            parts = [
                jnp.where(member, part[:, lanes], 0.0).astype(jnp.bfloat16)
                for part in (high, low)
            ]
            landed = one_hot_rows(BRICK_ROWS, rows_ref[at])
            return jnp.concatenate(parts, axis=0), landed

        def pair(j, ignored):
            both = [
                weigh(2 * j * per_tile + k, h) for k in range(2 * per_tile) for h in range(joined)
            ]
            carried = jnp.concatenate([first for first, _ in both], axis=1)
            landed = jnp.concatenate([second for _, second in both], axis=1)
            volume[...] += dot(carried, landed, NT)
            base = (g * segments + 2 * j * per_tile) * taken
            even[...] = product(2 * j)
            scatter(odd, base)
            odd[...] = product(2 * j + 1)
            scatter(even, base + per_tile * taken)
            return ignored

        return lax.fori_loop(0, tiles // 2, pair, ignored)

    lax.fori_loop(0, groups // joined, group, 0)
    scatter(odd, groups * segments * owned)
    span = map_ref.shape[2]

    def slots_of(i, parity):
        start = pl.multiple_of(brick_of(i, parity) * span, 8)
        return slots[pl.ds(start, span), :].astype(jnp.bfloat16)

    def keep(i, ignored):
        mine_ref[i] = slots_of(i, core)
        return ignored

    lax.fori_loop(0, bricks // 2, keep, 0)
    grid_bricks(1 - core, lambda i: slots_of(i, 1 - core), volume, map_ref, other_ref)


def brick_of(i, parity):
    chips = lax.axis_size("ori") // 2
    group = lax.bitwise_xor(lax.axis_index("img"), i // chips)
    chip = lax.bitwise_xor(lax.axis_index("ori") // 2, lax.rem(i, chips))
    return (group * chips + chip) * 2 + parity


def grid_bricks(parity, slots_of, volume, map_ref, out_ref):
    bricks = map_ref.shape[0]
    unroll = min(16, bricks // 2)
    sub = lax.broadcasted_iota(jnp.int32, (EXTRA_ROWS, 128), 0)

    def grid_brick(i):
        b = brick_of(i, parity)
        cells = dot(one_hot_rows(BRICK_ROWS, map_ref[b]), slots_of(i))
        out_ref[i, 0:BRICK_ROWS, :] = cells.astype(out_ref.dtype)
        total = volume[pl.ds(b, 1), :] + volume[pl.ds(bricks + b, 1), :]
        top = total.astype(jnp.bfloat16).astype(jnp.float32)
        rest = total - top
        extra = jnp.where(sub == 0, top[:, :128], jnp.where(sub == 1, top[:, 128:], 0.0))
        extra += jnp.where(sub == 2, rest[:, :128], jnp.where(sub == 3, rest[:, 128:], 0.0))
        out_ref[i, BRICK_ROWS : BRICK_ROWS + EXTRA_ROWS, :] = extra.astype(out_ref.dtype)

    def step(i, ignored):
        for k in range(unroll):
            grid_brick(i * unroll + k)
        return ignored

    lax.fori_loop(0, bricks // 2 // unroll, step, 0)


def grid_kernel(slots, volume, map_ref, out_ref):
    core = lax.rem(lax.axis_index("ori"), 2)
    grid_bricks(core, lambda i: slots[i], volume, map_ref, out_ref)


def grid_step(slots, volume, row_map):
    bricks = row_map.shape[0]
    shape = (bricks // 2, BRICK_ROWS + EXTRA_ROWS, 128)
    return pl.pallas_call(
        grid_kernel,
        out_shape=jax.ShapeDtypeStruct(shape, jnp.float32),
        in_specs=[VMEM] * 3,
        out_specs=VMEM,
        compiler_params=pltpu.CompilerParams(vmem_limit_bytes=8 << 20),
        cost_estimate=pl.CostEstimate(flops=1000, bytes_accessed=1000, transcendentals=0),
        name="grid_own_bricks",
    )(slots, volume, row_map)


def sum_step(bricks, groups, capacity, slot, p, stats, totals, x, dest, rows, row_map):
    blocks, orients, block = p.shape
    width = x.shape[1]
    owned = orients // groups
    joined = JOINED
    shape = (bricks // 2, BRICK_ROWS + EXTRA_ROWS, 128)
    return pl.pallas_call(
        functools.partial(sum_kernel, bricks, capacity),
        out_shape=[
            jax.ShapeDtypeStruct(shape, jnp.bfloat16),
            jax.ShapeDtypeStruct((bricks // 2, groups * capacity, 128), jnp.bfloat16),
            jax.ShapeDtypeStruct((2 * bricks, BRICK_ROWS), jnp.float32),
        ],
        in_specs=[SMEM] + [VMEM] * 7,
        out_specs=[VMEM] * 3,
        scratch_shapes=[
            pltpu.VMEM((joined * owned, blocks * block), jnp.bfloat16),
            pltpu.VMEM((joined * owned, TILE), jnp.float32),
            pltpu.VMEM((joined * owned, TILE), jnp.float32),
            pltpu.VMEM((bricks * groups * capacity + 512, 128), jnp.float32),
        ],
        compiler_params=pltpu.CompilerParams(vmem_limit_bytes=23 << 20),
        cost_estimate=pl.CostEstimate(
            flops=2 * blocks * block * orients * width, bytes_accessed=24 << 20, transcendentals=0
        ),
        name="sum_and_grid",
    )(slot, p, stats, totals, x, dest, rows, row_map)


def body(images, projections, brick_dest, brick_rows, kernel):
    image_groups = lax.axis_size("img")
    orient_groups = lax.axis_size("ori")
    chips = orient_groups // 2
    bricks = image_groups * orient_groups
    orients, segments = brick_rows.shape
    owned = orients // image_groups
    capacity = max(2, 2 * owned * segments // bricks)
    me = lax.axis_index("ori")

    swap = [(i, i ^ 1) for i in range(orient_groups)]
    along = [(i, i + 2) for i in range(0, orient_groups - 2, 2)]
    along += [(i + 2, i) for i in range(1, orient_groups - 2, 2)]

    with jax.named_scope("place_segments"):

        def lanes(values):
            values = values.reshape(image_groups, owned, segments).transpose(0, 2, 1)
            return values.reshape(image_groups * segments, 1, owned)

        dest, rows = lanes(brick_dest), lanes(brick_rows)
        room = max(128, capacity)
        slot, row_map = pl.pallas_call(
            functools.partial(place_kernel, bricks, image_groups, capacity),
            out_shape=[
                jax.ShapeDtypeStruct(dest.shape, jnp.int32),
                jax.ShapeDtypeStruct((image_groups, bricks, room), jnp.int32),
            ],
            in_specs=[VMEM, VMEM],
            out_specs=[VMEM, VMEM],
            compiler_params=pltpu.CompilerParams(vmem_limit_bytes=8 << 20),
            cost_estimate=pl.CostEstimate(flops=1000, bytes_accessed=1000, transcendentals=0),
            name="place_segments",
        )(dest, rows)
        row_map = row_map[:, :, :capacity].transpose(1, 0, 2).reshape(bricks, 1, image_groups * capacity)
        slot = slot.reshape(image_groups // JOINED, JOINED, segments, owned).transpose(0, 2, 1, 3)
        unused = jnp.full(
            ((TILE // 128) * JOINED * owned,), bricks * image_groups * capacity, jnp.int32
        )
        placed = (jnp.concatenate([unused, slot.reshape(-1)]), row_map, dest, rows)

    with jax.named_scope("score"):
        mate = lax.ppermute(images, "ori", swap)
        moving = [images, mate]
        mate, placed = lax.optimization_barrier((mate, placed))
        carry = score_step(
            chips, ((0, True, True), (0, True, False)), (images, mate), projections, None
        )

        def arrive(distance, q, part):
            own = q == 0
            both = (part, lax.ppermute(part, "ori", swap))
            return ((distance, True, own), (distance, False, not own)), both

        def score(waiting, carry):
            return score_step(chips, waiting[0], waiting[1], projections, carry)

        waiting = []
        for distance in range(1, chips):
            moving = [lax.ppermute(part, "ori", along) for part in moving]
            for q in range(2):
                if distance == 1:
                    moving[q], carry = lax.optimization_barrier((moving[q], carry))
                elif distance == 2 and q == 0:
                    moving[q], carry = lax.optimization_barrier((moving[q], carry))
                else:
                    carry = score(waiting.pop(0), carry)
                    if distance == chips - 1 and q == 1:
                        carry = score(waiting.pop(0), carry)
                    moving[q], carry = lax.optimization_barrier((moving[q], carry))
                waiting.append(arrive(distance, q, moving[q]))
        late = [sum(parts, ()) for parts in zip(*waiting)]
        carry = score(late, carry)
        _, p, x, stats = carry
        slot, row_map, dest, rows = placed

    with jax.named_scope("softmax_total"):
        totals = merge_step(stats, lax.ppermute(stats, "ori", swap))
        others = [
            lax.ppermute(totals, "ori", [(i, i ^ (2 * k)) for i in range(orient_groups)])
            for k in range(1, chips)
        ]
        totals = merge_step(totals, *others)

    with jax.named_scope("sum_and_grid"):
        other_cells, slots, volume = sum_step(
            bricks, image_groups, capacity, slot, p, stats, totals, x, dest, rows, row_map
        )

    with jax.named_scope("brick_sums"):
        height = BRICK_ROWS + EXTRA_ROWS

        def add_up(cells, axis, ways, stride):
            total = cells[0].astype(jnp.float32)
            for k in range(1, ways):
                perm = [(i, i ^ (k * stride)) for i in range(ways * stride)]
                part = cells[k].astype(jnp.bfloat16)
                total += lax.ppermute(part, axis, perm).astype(jnp.float32)
            return total

        other_cells = lax.ppermute(other_cells, "ori", swap)
        cells = grid_step(slots, volume, row_map)
        cells = cells + other_cells.astype(jnp.float32)
        cells = cells.reshape(image_groups, chips, height, 128)
        cells = add_up(cells, "img", image_groups, 1)
        cells = add_up(cells, "ori", chips, 2)

    gridded = cells[:BRICK_ROWS]
    data_volume = jnp.dot(gridded, kernel[0].astype(jnp.float32), precision=lax.Precision.HIGHEST)
    extra = cells[BRICK_ROWS:]
    weight_volume = (extra[0:2] + extra[2:4]).reshape(1, BRICK_ROWS)
    return (data_volume[None], weight_volume)


def solution(mesh):
    placed = (
        P(("img", "ori"), None),
        P("ori", None),
        P("ori", None, None),
        P("ori", None),
        P(("img", "ori"), None, None),
    )
    return jax.shard_map(
        body,
        mesh=mesh,
        in_specs=placed,
        out_specs=(P(("img", "ori"), None, None), P(("img", "ori"), None)),
        check_vma=False,
    )
```
